32 devices in a mesh: groups: 2 (over y), rep: 4 (over z), tp: 2 (over x), sub: 2 (over core).
Axes of the slice: x: 2, y: 2, z: 4, core: 2. Of those that a mesh axis runs over, the one named last changes fastest.
Arguments:
- rec_hidden: bfloat16 [8, 512, 5120], P(('groups', 'rep'), ('tp', 'sub')), parts along dimension 0
- dec_hidden: bfloat16 [8, 9, 2, 5120], P(('groups', 'rep')), parts along dimension 0
- norm_gain: float32 [5120], replicated, may hold values from 0.5 to 1.5
- query_gain: float32 [128], replicated, may hold values from 2 to 4
- key_gain: float32 [128], replicated, may hold values from 0.5 to 1.5
- w_query: bfloat16 [5120, 8192], P('rep', ('tp', 'sub')), may hold values from -0.078125 to 0.078125
- w_key: bfloat16 [5120, 1024], P('rep', ('tp', 'sub')), may hold values from -0.078125 to 0.078125
- w_value: bfloat16 [5120, 1024], P('rep', ('tp', 'sub')), may hold values from -0.078125 to 0.078125
- pool_keys: bfloat16 [8, 40, 128, 1024], P(('groups', 'rep'), None, None, ('tp', 'sub')), parts along dimension 0, may hold values from -1.5 to 1.5
- pool_values: bfloat16 [8, 40, 128, 1024], P(('groups', 'rep'), None, None, ('tp', 'sub')), parts along dimension 0, may hold values from -6 to 6
- page_table: int32 [8, 8, 16], P(('groups', 'rep')), parts along dimension 0, may hold values from 0 to 39, as said below
- seq_lengths: int32 [8, 8], P('groups'), parts along dimension 0, may hold values from 0 to 2048, as said below
- listed_slot: int32 [8], P('groups'), parts along dimension 0, may hold values from 0 to 7
Outputs:
- rec_keys: bfloat16 [8, 512, 1024], P(('groups', 'rep'), None, ('tp', 'sub')), parts along dimension 0
- rec_values: bfloat16 [8, 512, 1024], P(('groups', 'rep'), None, ('tp', 'sub')), parts along dimension 0
- decoded: bfloat16 [8, 9, 2, 8192], P(('groups', 'rep'), None, None, ('tp', 'sub')), parts along dimension 0
The draws below stay inside these ranges and needn't reach their ends.
There are 2 independent parts, one for each index of `groups`. The reference program is written for one: setup_inputs(seed, part) draws one part's arguments, and reference() takes and returns one part's arrays. A program takes and returns all parts, laid end to end along the dimension named above; an argument that names none is the same for every part. Nothing has to cross between parts.
Inputs may be any that keep to these rules, and one draw needn't show every extreme that they name: `seq_lengths`: the listed sequence of a replica r < 2 holds more than (14) * 128 tokens, the listed slot of any other replica holds 0; every other sequence holds 1 to 384 tokens. `page_table`: the first ceil(length / 128) entries of a sequence's row name pages of the replica's own pool, distinct over all sequences of the replica; the other entries name arbitrary pages of that pool.
All inputs are finite; a program needn't handle non-finite values.
Results may differ from the reference program's by a relative error of at most 0.0092.
Values may be sent and summed in bfloat16 or wider, within the bound.
No kernel may reach another device: no remote copies, remote signals or barrier semaphores. Data moves between devices by JAX's collectives and lax.ppermute only.
A program may use at most 128 MiB of HBM per device.

```python
import math
import jax
import jax.numpy as jnp
from jax import lax

D = 5120
QH = 64
KVH = 8
HD = 128
PAGE = 128
PPS = 16
KEEP_PAGES = 3
STEPS = 2
NSEQ = 8
REC_LEN = 512
REPLICAS = 4
POOL = 40


def spread_scales(key, shape):
    row_key, column_key = jax.random.split(key)
    row_scale = 10.0 ** jax.random.uniform(row_key, shape[:-1] + (1,), jnp.float32)
    column_scale = 10.0 ** jax.random.uniform(column_key, (shape[-1],), jnp.float32)
    return row_scale * column_scale * 0.1


def scaled_states(base, scale_key):
    return (base * spread_scales(scale_key, base.shape)).astype(jnp.bfloat16)


def draw_rec_hidden(key, part):
    key = jax.random.fold_in(key, 11)
    shape = (REPLICAS, REC_LEN, D)
    base_key, scale_key = jax.random.split(key)
    base = jax.random.normal(base_key, shape, jnp.float32)
    return scaled_states(base, scale_key)


def draw_dec_hidden(key, part):
    key = jax.random.fold_in(key, 13)
    shape = (REPLICAS, NSEQ + 1, STEPS, D)
    base_key, scale_key = jax.random.split(key)
    base = jax.random.normal(base_key, shape, jnp.float32)
    return scaled_states(base, scale_key)


def layout(key):
    listed_key, kept_key, longest_key, order_key, top_key, bottom_key = jax.random.split(jax.random.fold_in(key, 5), 6)
    replica_ids = jnp.arange(REPLICAS, dtype=jnp.int32)
    slot_ids = jnp.arange(NSEQ, dtype=jnp.int32)
    listed = jax.random.randint(listed_key, (REPLICAS,), 0, NSEQ, jnp.int32)
    top_replica = jax.random.randint(top_key, (), 0, REPLICAS, jnp.int32)
    bottom_replica = (top_replica + jax.random.randint(bottom_key, (), 1, REPLICAS, jnp.int32)) % REPLICAS
    listed = jnp.where(replica_ids == top_replica, NSEQ - 1, listed)
    listed = jnp.where(replica_ids == bottom_replica, 0, listed).astype(jnp.int32)
    kept = jax.random.randint(kept_key, (REPLICAS, NSEQ), 1, KEEP_PAGES * PAGE + 1, jnp.int32)
    forced = (slot_ids[None, :] == (listed[0] + 1) % NSEQ) & (replica_ids[:, None] == 0)
    kept = jnp.where(forced, KEEP_PAGES * PAGE, kept)
    longest = jax.random.randint(longest_key, (REPLICAS,), (PPS - 2) * PAGE + 1, PPS * PAGE + 1, jnp.int32)
    longest = jnp.where(replica_ids == 0, PPS * PAGE, longest)
    at_listed = slot_ids[None, :] == listed[:, None]
    busy_rows = (replica_ids < REPLICAS // 2)[:, None]
    lengths = jnp.where(at_listed, jnp.where(busy_rows, longest[:, None], 0), kept).astype(jnp.int32)
    ranks = jax.random.randint(order_key, (REPLICAS, POOL), 0, 1 << 20, jnp.int32) * POOL + jnp.arange(POOL, dtype=jnp.int32)[None, :]
    order = jnp.argsort(ranks, axis=1, stable=True).astype(jnp.int32)
    page_ids = jnp.arange(PPS, dtype=jnp.int32)
    kept_rank = slot_ids[None, :] - (slot_ids[None, :] > listed[:, None]).astype(jnp.int32)
    index = jnp.where(at_listed[:, :, None], page_ids[None, None, :], PPS + kept_rank[:, :, None] * KEEP_PAGES + page_ids[None, None, :]) % POOL
    table = jnp.take_along_axis(order, index.reshape(REPLICAS, NSEQ * PPS), axis=1).reshape(REPLICAS, NSEQ, PPS)
    return (listed, lengths, table.astype(jnp.int32))


def draw_listed_slot(key, part):
    listed, lengths, table = layout(key)
    return listed


def draw_seq_lengths(key, part):
    listed, lengths, table = layout(key)
    return lengths


def draw_page_table(key, part):
    listed, lengths, table = layout(key)
    return table


def steps_of(rng, dims, shards, low, largest):
    factor_of, own = 1.0, jax.random.fold_in(rng, 6)
    for axis_at, parts in shards:
        draws = jnp.exp(jax.random.uniform(jax.random.fold_in(own, axis_at), (parts,), jnp.float32, low / len(shards), largest / len(shards)))
        factor_of = factor_of * jnp.repeat(draws, dims[axis_at] // parts).reshape([-1 if axis == axis_at else 1 for axis in range(len(dims))])
    return factor_of


def bell_draw(stream_key, dims, scale, limit, pieces=(), held_as=jnp.bfloat16):
    factor_of = steps_of(stream_key, dims, pieces, -0.22, 0.18) if pieces else 1.0
    values = jax.random.normal(stream_key, dims, jnp.float32) * scale * factor_of
    return jnp.minimum(jnp.maximum(values, -limit), limit).astype(held_as)


def setup_inputs(seed: int = 0, part: int = 0) -> dict:
    key_of = jax.random.split(jax.random.key(seed), 14)
    own_keys = jax.random.split(jax.random.fold_in(key_of[13], part), 14)
    rec_hidden = draw_rec_hidden(jax.random.fold_in(jax.random.fold_in(key_of[13], part), 71), part)
    dec_hidden = draw_dec_hidden(jax.random.fold_in(jax.random.fold_in(key_of[13], part), 71), part)
    norm_gain = jnp.clip(1.0 + 0.1 * jax.random.normal(key_of[2], (D,), jnp.float32), 0.5, 1.5)
    query_gain = jnp.clip(jax.random.uniform(key_of[3], (HD,), jnp.float32, 2.0, 4.0), 2.0, 4.0)
    key_gain = jnp.clip(1.0 + 0.1 * jax.random.normal(key_of[4], (HD,), jnp.float32), 0.5, 1.5)
    w_query = bell_draw(key_of[5], (D, QH * HD), D ** -0.5, 0.078125, ((0, 4), (1, 4)))
    w_key = bell_draw(key_of[6], (D, KVH * HD), D ** -0.5, 0.078125, ((0, 4), (1, 4)))
    w_value = bell_draw(key_of[7], (D, KVH * HD), D ** -0.5, 0.078125, ((0, 4), (1, 4)))
    pool_keys = jnp.clip(jax.random.uniform(own_keys[8], (REPLICAS, POOL, PAGE, KVH * HD), jnp.float32, -1.5, 1.5) * steps_of(own_keys[8], (REPLICAS, POOL, PAGE, KVH * HD), ((0, 4), (3, 4)), -0.4, 0.0), -1.5, 1.5).astype(jnp.bfloat16)
    pool_values = bell_draw(own_keys[9], (REPLICAS, POOL, PAGE, KVH * HD), 1.0, 6.0, ((0, 4), (3, 4)))
    page_table = draw_page_table(jax.random.fold_in(jax.random.fold_in(key_of[13], part), 71), part)
    seq_lengths = draw_seq_lengths(jax.random.fold_in(jax.random.fold_in(key_of[13], part), 71), part)
    listed_slot = draw_listed_slot(jax.random.fold_in(jax.random.fold_in(key_of[13], part), 71), part)
    return dict(rec_hidden=rec_hidden, dec_hidden=dec_hidden, norm_gain=norm_gain, query_gain=query_gain, key_gain=key_gain, w_query=w_query, w_key=w_key, w_value=w_value, pool_keys=pool_keys, pool_values=pool_values, page_table=page_table, seq_lengths=seq_lengths, listed_slot=listed_slot)


EPSILON = 1e-06
ROPE_BASE = 1000000.0

def normalize(states, gain):
    values = states.astype(jnp.float32)
    scale = lax.rsqrt(lax.optimization_barrier(jnp.mean(values * values, axis=-1, keepdims=True)) + EPSILON)
    return (values * scale * gain).astype(jnp.bfloat16)

def head_norm(values, gain):
    scale = lax.rsqrt(lax.optimization_barrier(jnp.mean(values * values, axis=-1, keepdims=True)) + EPSILON)
    return values * scale * gain

def rotate(values, positions):
    half_size = values.shape[-1] // 2
    freqs = jnp.exp(jnp.arange(half_size, dtype=jnp.float32) * (-2.0 * math.log(ROPE_BASE) / values.shape[-1]))
    angles = positions.astype(jnp.float32)[:, None] * freqs[None, :]
    cosine = jnp.cos(angles)[:, None, :]
    sine = jnp.sin(angles)[:, None, :]
    first = values[..., :half_size]
    second = values[..., half_size:]
    return jnp.concatenate([first * cosine - second * sine, second * cosine + first * sine], axis=-1)

def keys_values(normed, weight_key, weight_value, key_gain, positions):
    rows = normed.shape[0]
    raw = jnp.dot(normed, weight_key, preferred_element_type=jnp.float32)
    heads = raw.reshape(rows, -1, key_gain.shape[0])
    keys = rotate(head_norm(heads, key_gain), positions).reshape(rows, -1).astype(jnp.bfloat16)
    values = jnp.dot(normed, weight_value, preferred_element_type=jnp.float32).astype(jnp.bfloat16)
    return (keys, values)

def queries_from(projected, query_gain, positions):
    rows = projected.shape[0]
    heads = projected.reshape(rows, -1, query_gain.shape[0])
    rotated = rotate(head_norm(heads, query_gain), positions)
    return (rotated * query_gain.shape[0] ** (-0.5)).reshape(rows, -1).astype(jnp.bfloat16)

def rounded(values):
    return lax.optimization_barrier(values.astype(jnp.bfloat16)).astype(jnp.float32)

def attend(queries, cache_keys, cache_values, new_keys, new_values, base_length):
    slots, steps, query_cols = queries.shape
    context = cache_keys.shape[1]
    kv_heads = cache_keys.shape[2] // HD
    groups = query_cols // cache_keys.shape[2]
    grouped = queries.reshape(slots, steps, kv_heads, groups, HD).astype(jnp.float32)
    stored_keys = cache_keys.reshape(slots, context, kv_heads, HD).astype(jnp.float32)
    stored_values = cache_values.reshape(slots, context, kv_heads, HD).astype(jnp.float32)
    fresh_keys = new_keys.reshape(slots, steps, kv_heads, HD).astype(jnp.float32)
    fresh_values = new_values.reshape(slots, steps, kv_heads, HD).astype(jnp.float32)
    old_scores = jnp.einsum('stkgd,sckd->stkgc', grouped, stored_keys)
    new_scores = jnp.einsum('stkgd,sukd->stkgu', grouped, fresh_keys)
    old_mask = (jnp.arange(context, dtype=jnp.int32)[None, :] < base_length[:, None])[:, None, None, None, :]
    step_ids = jnp.arange(steps, dtype=jnp.int32)
    new_mask = (step_ids[None, :] <= step_ids[:, None])[None, :, None, None, :]
    old_exp = jnp.where(old_mask, jnp.exp(old_scores), jnp.float32(0.0))
    new_exp = jnp.where(new_mask, jnp.exp(new_scores), jnp.float32(0.0))
    total = lax.optimization_barrier(jnp.sum(old_exp, axis=-1, keepdims=True)) + lax.optimization_barrier(jnp.sum(new_exp, axis=-1, keepdims=True))
    old_weights = rounded(old_exp / total)
    new_weights = rounded(new_exp / total)
    mixed = jnp.einsum('stkgc,sckd->stkgd', old_weights, stored_values)
    mixed = mixed + jnp.einsum('stkgu,sukd->stkgd', new_weights, fresh_values)
    return mixed.reshape(slots, steps, kv_heads * groups * HD)

def reference(rec_hidden, dec_hidden, norm_gain, query_gain, key_gain, w_query, w_key, w_value, pool_keys, pool_values, page_table, seq_lengths, listed_slot):
    half_count = REPLICAS // 2
    context = PPS * PAGE

    def one_replica(replica):
        partner = (replica + half_count) % REPLICAS
        is_busy = replica < half_count
        normed_rec = normalize(rec_hidden[replica], norm_gain)
        rec_k, rec_v = keys_values(normed_rec, w_key, w_value, key_gain, jnp.arange(REC_LEN, dtype=jnp.int32))
        mine = listed_slot[replica]
        theirs = listed_slot[partner]
        at_listed = jnp.arange(NSEQ, dtype=jnp.int32) == mine
        moved_length = seq_lengths[partner, theirs]
        slot_length = jnp.where(at_listed, jnp.where(is_busy, 0, moved_length), seq_lengths[replica]).astype(jnp.int32)
        base_length = jnp.concatenate([slot_length, jnp.full((1,), REC_LEN, jnp.int32)])
        live = jnp.where(at_listed & is_busy, jnp.float32(0.0), jnp.float32(1.0))
        live = jnp.concatenate([live, jnp.ones((1,), jnp.float32)])
        take_moved = (at_listed & jnp.logical_not(is_busy))[:, None, None]
        own_k = pool_keys[replica][page_table[replica]].reshape(NSEQ, context, -1)
        own_v = pool_values[replica][page_table[replica]].reshape(NSEQ, context, -1)
        moved_k = pool_keys[partner][page_table[partner, theirs]].reshape(context, -1)
        moved_v = pool_values[partner][page_table[partner, theirs]].reshape(context, -1)
        padding = jnp.zeros((context - REC_LEN, rec_k.shape[1]), jnp.bfloat16)
        cache_k = jnp.concatenate([jnp.where(take_moved, moved_k[None], own_k), jnp.concatenate([rec_k, padding])[None]])
        cache_v = jnp.concatenate([jnp.where(take_moved, moved_v[None], own_v), jnp.concatenate([rec_v, padding])[None]])
        positions = (base_length[:, None] + jnp.arange(STEPS, dtype=jnp.int32)[None, :]).reshape(-1)
        normed_new = normalize(dec_hidden[replica].reshape(-1, D), norm_gain)
        new_k, new_v = keys_values(normed_new, w_key, w_value, key_gain, positions)
        queries = queries_from(jnp.dot(normed_new, w_query, preferred_element_type=jnp.float32), query_gain, positions)
        slots = NSEQ + 1
        mixed = attend(queries.reshape(slots, STEPS, -1), cache_k, cache_v, new_k.reshape(slots, STEPS, -1), new_v.reshape(slots, STEPS, -1), base_length)
        decoded = (mixed * live[:, None, None]).astype(jnp.bfloat16)
        return (rec_k, rec_v, decoded)
    rec_keys, rec_values, decoded = lax.map(one_replica, jnp.arange(REPLICAS, dtype=jnp.int32))
    return (rec_keys, rec_values, decoded)
```

```python
import functools
import math

import jax
import jax.numpy as jnp
from jax import lax
from jax.experimental import pallas as pl
from jax.experimental.pallas import tpu as pltpu
from jax.sharding import PartitionSpec as P

EPSILON = 1e-06
ROPE_BASE = 1000000.0
KEEP_PAGES = 3
VMEM_BYTES = 56 * 2**20
F32 = jnp.float32
BF16 = jnp.bfloat16

WHOLE = pl.BlockSpec(memory_space=pltpu.VMEM)
SCALAR = pl.BlockSpec(memory_space=pltpu.SMEM)


def call(kernel, outs, ins, scalars, scratch=(), flops=0, **grid):
    bytes_accessed = sum(math.prod(a.shape) * a.dtype.itemsize for a in list(ins) + list(outs))
    return pl.pallas_call(
        kernel,
        out_shape=tuple(outs),
        in_specs=[SCALAR] * len(scalars) + [WHOLE] * len(ins),
        out_specs=tuple([WHOLE] * len(outs)),
        scratch_shapes=list(scratch),
        compiler_params=pltpu.CompilerParams(vmem_limit_bytes=VMEM_BYTES),
        cost_estimate=pl.CostEstimate(flops=flops, bytes_accessed=bytes_accessed, transcendentals=0),
    )(*scalars, *ins)


def shaped(shape, dtype):
    return jax.ShapeDtypeStruct(shape, dtype)


def dot(a, b):
    return jnp.dot(a, b, preferred_element_type=F32)


def dot_rows(a, b):
    return lax.dot_general(a, b, (((1,), (1,)), ((), ())), preferred_element_type=F32)


def xor_permute(value, axis, distance):
    count = lax.axis_size(axis)
    return lax.ppermute(value, axis, [(i, i ^ distance) for i in range(count)])


def head_scale(values):
    return lax.rsqrt(jnp.mean(values * values, axis=-1, keepdims=True) + EPSILON)


def rotate_rows(values, cosine, sine):
    return values * cosine + pltpu.roll(values, values.shape[-1] // 2, values.ndim - 1) * sine


def rope_tables(positions, head_size):
    half_size = head_size // 2
    freqs = jnp.exp(jnp.arange(half_size, dtype=F32) * (-2.0 * math.log(ROPE_BASE) / head_size))
    angles = positions.astype(F32)[:, None] * freqs[None, :]
    cosine, sine = jnp.cos(angles), jnp.sin(angles)
    return jnp.concatenate([cosine, cosine], axis=1), jnp.concatenate([-sine, sine], axis=1)


def normalize(states, gain):
    values = states.astype(F32)
    return (values * head_scale(values) * gain).astype(BF16)


def norm_spread_kernel(x_ref, gain_ref, *outs):
    replica = lax.axis_index("rep")
    width = outs[0].shape[1]
    values = x_ref[...].astype(F32)
    scale = head_scale(values)
    for k, out in enumerate(outs):
        at = pl.multiple_of((replica ^ k) * width, 128)
        part = x_ref[:, pl.ds(at, width)].astype(F32)
        out[...] = (part * scale * gain_ref[:, pl.ds(at, width)]).astype(BF16)


def project_kernel(count, slots, steps, listed_ref, *refs):
    rows = refs[:count]
    wq_ref, wk_ref, wv_ref = refs[count : count + 3]
    outs = refs[count + 3 : 2 * count + 3]
    stacked = refs[2 * count + 3]
    replica = lax.axis_index("rep")
    half = count // 2
    step = pl.program_id(0)
    per = slots * steps

    @pl.when(step == 0)
    def _():
        for k in range(count):
            own = rows[k][...].astype(F32)
            other = rows[k ^ half][...].astype(F32)
            busy = (replica ^ k) < half
            mine = listed_ref[replica ^ k]
            theirs = listed_ref[replica ^ k ^ half]
            ids = lax.broadcasted_iota(jnp.int32, (per, 1), 0)
            for t in range(steps):
                moved = jnp.sum(jnp.where(ids == theirs * steps + t, other, 0.0), axis=0, keepdims=True)
                own = jnp.where((ids == mine * steps + t) & busy, moved, own)
            stacked[k, :per, :] = own.astype(BF16)

    lhs = stacked[...].reshape(-1, stacked.shape[2])
    pad = stacked.shape[1]
    last = pl.num_programs(0) - 1

    @pl.when(step < last)
    def _():
        product = dot(lhs, wq_ref[...])
        for k in range(count):
            outs[k][...] = product[k * pad : k * pad + per].astype(outs[k].dtype)

    @pl.when(step == last)
    def _():
        product = jnp.concatenate([dot(lhs, wk_ref[...]), dot(lhs, wv_ref[...])], axis=1)
        for k in range(count):
            outs[k][...] = product[k * pad : k * pad + per].astype(outs[k].dtype)


def project_new(rows, listed, w_query, w_key, w_value, slots, steps):
    count = len(rows)
    per, depth = rows[0].shape
    block = 2 * w_key.shape[1]
    blocks = w_query.shape[1] // block
    pad = -(-per // 16) * 16
    total = w_query.shape[1] + block
    return pl.pallas_call(
        functools.partial(project_kernel, count, slots, steps),
        grid=(blocks + 1,),
        out_shape=tuple(shaped((per, total), F32) for _ in rows),
        in_specs=[SCALAR]
        + [pl.BlockSpec((per, depth), lambda j: (0, 0)) for _ in rows]
        + [
            pl.BlockSpec((depth, block), lambda j: (0, jnp.minimum(j, blocks - 1))),
            pl.BlockSpec(w_key.shape, lambda j: (0, 0)),
            pl.BlockSpec(w_value.shape, lambda j: (0, 0)),
        ],
        out_specs=tuple(pl.BlockSpec((per, block), lambda j: (0, j)) for _ in rows),
        scratch_shapes=[pltpu.VMEM((count, pad, depth), BF16)],
        compiler_params=pltpu.CompilerParams(vmem_limit_bytes=VMEM_BYTES),
        cost_estimate=pl.CostEstimate(
            flops=2 * count * per * depth * total, bytes_accessed=2 * depth * total, transcendentals=0
        ),
    )(listed, *rows, w_query, w_key, w_value)


def spread_heads(rows, kv_heads):
    heads = kv_heads * 8
    ids = lax.broadcasted_iota(jnp.int32, (rows.shape[0], 1), 0) % heads // 8
    return jnp.concatenate([jnp.where(ids == k, rows, 0.0) for k in range(kv_heads)], axis=1)


def own_head(wide, kv_heads):
    size = wide.shape[1] // kv_heads
    heads = kv_heads * 8
    ids = lax.broadcasted_iota(jnp.int32, (wide.shape[0], 1), 0) % heads // 8
    total = wide[:, :size]
    for k in range(1, kv_heads):
        total = jnp.where(ids == k, wide[:, k * size : (k + 1) * size], total)
    return total


def attend_kernel(parts, seq_count, steps, table_ref, lengths_ref, listed_ref, *refs):
    sums = refs[:parts]
    (cos_ref, sin_ref, qgain_ref, kgain_ref, keys_ref, values_ref) = refs[parts : parts + 6]
    num_ref, den_ref, moved_ref, last_ref = refs[parts + 6 : parts + 10]
    q3, k3, v3 = refs[parts + 10 :]
    replica = lax.axis_index("rep")
    half = lax.axis_size("rep") // 2
    size = qgain_ref.shape[1]
    width = keys_ref.shape[2]
    page = keys_ref.shape[1]
    kv_heads = width // size
    heads = kv_heads * 8
    slots = seq_count + 1

    def total(at):
        value = sums[0][:, at : at + size].astype(F32)
        for other in sums[1:]:
            value = value + other[:, at : at + size].astype(F32)
        return value

    cosine, sine = cos_ref[...], sin_ref[...]
    for h in range(heads):
        x = total(h * size)
        x = rotate_rows(x * head_scale(x) * qgain_ref[...], cosine, sine) * size**-0.5
        q3[:, h, :] = x.astype(BF16).astype(F32)
    for h in range(kv_heads):
        x = total((heads + h) * size)
        x = rotate_rows(x * head_scale(x) * kgain_ref[...], cosine, sine).astype(BF16).astype(F32)
        k3[:, h * 8 : h * 8 + 8, :] = jnp.broadcast_to(x[:, None, :], (x.shape[0], 8, size))
        v = total((heads + kv_heads + h) * size).astype(BF16).astype(F32)
        v3[:, h * 8 : h * 8 + 8, :] = jnp.broadcast_to(v[:, None, :], (x.shape[0], 8, size))

    def old_terms(rows, page_of, length, pages, first):
        num, den = None, None
        for i in range(pages):
            at = first + i
            scores = dot_rows(rows, keys_ref[page_of(at)])
            ids = lax.broadcasted_iota(jnp.int32, scores.shape, 1) + at * page
            weights = jnp.where(ids < length, jnp.exp(scores), 0.0)
            part = jnp.sum(weights, axis=-1, keepdims=True)
            mixed = dot(weights.astype(BF16), values_ref[page_of(at)])
            num = mixed if num is None else num + mixed
            den = part if den is None else den + part
        return num, den

    def rows_of(slot):
        return q3[pl.ds(slot * steps, steps)].reshape(steps * heads, size)

    for slot in range(slots):
        q = q3[slot * steps : (slot + 1) * steps]
        k = k3[slot * steps : (slot + 1) * steps]
        v = v3[slot * steps : (slot + 1) * steps]
        nums, dens = [], []
        for t in range(steps):
            num, den = None, None
            for u in range(t + 1):
                e = jnp.exp(jnp.sum(q[t] * k[u], axis=-1, keepdims=True))
                num = e * v[u] if num is None else num + e * v[u]
                den = e if den is None else den + e
            nums.append(num)
            dens.append(den)
        num, den = jnp.concatenate(nums, axis=0), jnp.concatenate(dens, axis=0)
        rows = spread_heads(rows_of(slot), kv_heads).astype(BF16)
        if slot < seq_count:
            old_num, old_den = old_terms(
                rows, lambda at: table_ref[slot, at], lengths_ref[replica, slot], KEEP_PAGES, 0
            )
            num = num + own_head(old_num, kv_heads)
            den = den + old_den
        else:
            last_ref[...] = rows
        num_ref[slot * steps : (slot + 1) * steps] = num.reshape(steps, heads, size)
        den_ref[slot * steps : (slot + 1) * steps] = jnp.broadcast_to(den, num.shape).reshape(
            steps, heads, size
        )

    moved_ref[...] = jnp.zeros_like(moved_ref)

    @pl.when(replica < half)
    def _():
        slot = listed_ref[replica]
        length = lengths_ref[replica, slot]
        rows = spread_heads(rows_of(slot), kv_heads).astype(BF16)
        pages = table_ref.shape[1]
        at_once = 4

        def turn(i, carry):
            num, den = old_terms(rows, lambda at: table_ref[slot, at], length, at_once, i * at_once)
            return carry[0] + num, carry[1] + den

        num, den = lax.fori_loop(
            0,
            pages // at_once,
            turn,
            (jnp.zeros((steps * heads, width), F32), jnp.zeros((steps * heads, 1), F32)),
        )
        num = own_head(num, kv_heads)
        moved_ref[0] = num
        moved_ref[1] = jnp.broadcast_to(den, num.shape)


def norm_blocks_kernel(x_ref, gain_ref, out_ref):
    width = out_ref.shape[2]
    values = x_ref[...].astype(F32)
    scale = head_scale(values)
    for k, at in enumerate(half_blocks()):
        at = pl.multiple_of(at * width, 128)
        part = x_ref[:, pl.ds(at, width)].astype(F32)
        out_ref[k] = (part * scale * gain_ref[:, pl.ds(at, width)]).astype(BF16)


def half_blocks():
    replica, group = lax.axis_index("rep"), lax.axis_index("groups")
    second = jnp.where(replica < 2, 2, 1)
    third = jnp.where(replica < 2, 3, 0)
    order = [2 * replica, 2 * replica + 1]
    for source in (replica ^ 1, second, third):
        order += [2 * source + group, 2 * source + 1 - group]
    return order


def first_kernel(*refs):
    xs = refs[:4]
    wk_ref, wv_ref, a_ref, ya_ref, b_ref, c_ref, yb_ref, yc_ref, acc_ref = refs[4:]
    replica = lax.axis_index("rep")
    middle = (replica == 1) | (replica == 2)
    width = wk_ref.shape[1]
    depth = a_ref.shape[0]

    def block(k):
        return jnp.concatenate([x[k] for x in xs], axis=0)

    keys, values = None, None
    for k in range(2):
        x = block(k)
        more_k = dot(x, wk_ref[k * depth : (k + 1) * depth])
        more_v = dot(x, wv_ref[k * depth : (k + 1) * depth])
        keys = more_k if keys is None else keys + more_k
        values = more_v if values is None else values + more_v
    acc_ref[:, :width] = keys
    acc_ref[:, width:] = values
    acc_ref[...] += dot(block(2), a_ref[...])
    acc_ref[...] += dot(block(3), ya_ref[...])

    @pl.when(middle)
    def _():
        acc_ref[...] += dot(block(4), b_ref[...])
        acc_ref[...] += dot(block(5), yb_ref[...])

    @pl.when(jnp.logical_not(middle))
    def _():
        acc_ref[...] += dot(block(4), c_ref[...])
        acc_ref[...] += dot(block(5), yc_ref[...])


def tail_kernel(far, steps, listed_ref, *refs):
    if far:
        xs, (d_ref, e_ref, yd_ref, ye_ref) = refs[:4], refs[4:8]
        refs = refs[8:]
    acc_ref, cos_ref, sin_ref, kgain_ref, rows_ref, num_ref, den_ref, moved_ref = refs[:8]
    keys_ref, values_ref, out_ref, o3 = refs[8:12]
    replica = lax.axis_index("rep")
    half = lax.axis_size("rep") // 2
    tokens, width = keys_ref.shape
    size = kgain_ref.shape[1]
    kv_heads = width // size
    heads = kv_heads * 8
    slots = num_ref.shape[0] // steps

    if far:
        fresh = refs[12]
        middle = (replica == 1) | (replica == 2)

        def block(k):
            return jnp.concatenate([x[k] for x in xs], axis=0)

        @pl.when(middle)
        def _():
            fresh[...] = acc_ref[...] + dot(block(6), d_ref[...]) + dot(block(7), yd_ref[...])

        @pl.when(jnp.logical_not(middle))
        def _():
            fresh[...] = acc_ref[...] + dot(block(6), e_ref[...]) + dot(block(7), ye_ref[...])

        tp, sub = lax.axis_index("tp"), lax.axis_index("sub")
        places = [tp * 2 + sub, (tp ^ 1) * 2 + sub, tp * 2 + (sub ^ 1), (tp ^ 1) * 2 + (sub ^ 1)]
    else:
        fresh, places = acc_ref, [0]
    chunk = tokens // len(places)
    for i, place in enumerate(places):
        if len(places) > 1:
            place = pl.ds(pl.multiple_of(place * chunk, chunk), chunk)
        else:
            place = pl.ds(0, chunk)
        cosine, sine = cos_ref[place, :], sin_ref[place, :]
        for h in range(kv_heads):
            x = fresh[i * chunk : (i + 1) * chunk, h * size : (h + 1) * size]
            x = rotate_rows(x * head_scale(x) * kgain_ref[...], cosine, sine)
            keys_ref[place, h * size : (h + 1) * size] = x.astype(BF16)
        values_ref[place, :] = fresh[i * chunk : (i + 1) * chunk, width:].astype(BF16)

    weights = jnp.exp(dot_rows(rows_ref[...], keys_ref[...]))
    old_num = own_head(dot(weights.astype(BF16), values_ref[...]), kv_heads)
    old_den = jnp.sum(weights, axis=-1, keepdims=True)
    at = (slots - 1) * steps
    o3[:at] = num_ref[:at] / den_ref[:at]
    o3[at:] = (num_ref[at:] + old_num.reshape(steps, heads, size)) / (
        den_ref[at:] + jnp.broadcast_to(old_den, old_num.shape).reshape(steps, heads, size)
    )
    mine = pl.ds(listed_ref[replica] * steps, steps)
    live = jnp.where(replica < half, 0.0, 1.0)
    o3[mine] = (
        live
        * (num_ref[mine] + moved_ref[0].reshape(steps, heads, size))
        / (den_ref[mine] + moved_ref[1].reshape(steps, heads, size))
    )
    for h in range(heads):
        out_ref[:, h * size : (h + 1) * size] = o3[:, h, :].astype(BF16)


def line_pairs(pairs, axis="rep"):
    return lambda value: lax.ppermute(value, axis, pairs)


def across_groups(value, replicas):
    count = lax.axis_size("rep")
    pairs = [(g * count + r, (1 - g) * count + r) for g in range(2) for r in replicas]
    return lax.ppermute(value, ("groups", "rep"), pairs)


def body(
    rec_hidden,
    dec_hidden,
    norm_gain,
    query_gain,
    key_gain,
    w_query,
    w_key,
    w_value,
    pool_keys,
    pool_values,
    page_table,
    seq_lengths,
    listed_slot,
):
    replicas = lax.axis_size("rep")
    half = replicas // 2
    replica = lax.axis_index("rep")
    partner = (replica + half) % replicas
    head_size = query_gain.shape[0]
    width = w_key.shape[1]
    depth = w_key.shape[0]
    _, slots, steps, features = dec_hidden.shape
    seq_count = slots - 1
    per = slots * steps
    heads = w_query.shape[1] // head_size
    gain = norm_gain[None]
    qgain, kgain = query_gain[None], key_gain[None]
    table = page_table[0]
    tokens = rec_hidden.shape[1] * lax.axis_size("tp") * lax.axis_size("sub")
    near = (
        replicas == 4
        and lax.axis_size("tp") == 2
        and lax.axis_size("sub") == 2
        and lax.axis_size("groups") == 2
    )

    if near:
        group = lax.axis_index("groups")
        rows = depth // 2
        own = jnp.concatenate(
            [lax.dynamic_slice_in_dim(w, group * rows, rows, 0) for w in (w_key, w_value)], axis=1
        )
        from_a = line_pairs([(0, 1), (1, 0), (2, 3), (3, 2)])(own)
        from_b = line_pairs([(1, 2), (2, 1)])(own)

    hidden = dec_hidden[0].reshape(per, features)
    if near:
        spread = call(
            norm_spread_kernel, [shaped((per, depth), BF16)] * replicas, [hidden, gain], []
        )
        spread = [spread[0]] + [xor_permute(spread[k], "rep", k) for k in range(1, replicas)]
        sums = project_new(spread, listed_slot, w_query, w_key, w_value, slots, steps)
        sums = [sums[0]] + [xor_permute(sums[k], "rep", k) for k in range(1, replicas)]
    else:
        spread = lax.all_to_all(
            normalize(hidden, norm_gain), "rep", split_axis=1, concat_axis=0, tiled=True
        ).reshape(replicas, slots, steps, depth)
        moved = jnp.take_along_axis(spread, listed_slot[:, None, None, None], axis=1)
        moved = jnp.roll(moved, half, axis=0)
        ids = jnp.arange(replicas)[:, None]
        swap = (jnp.arange(slots)[None] == listed_slot[:, None]) & (ids < half)
        spread = jnp.where(swap[:, :, None, None], moved, spread).reshape(replicas * per, depth)
        weights = jnp.concatenate([w_query, w_key, w_value], axis=1)
        sums = [
            lax.psum_scatter(
                jnp.dot(spread, weights, preferred_element_type=F32),
                "rep",
                scatter_dimension=0,
                tiled=True,
            )
        ]

    rec_cos, rec_sin = rope_tables(jnp.arange(tokens, dtype=jnp.int32), head_size)
    if near:
        (blocks,) = call(
            norm_blocks_kernel,
            [shaped((2 * replicas, rec_hidden.shape[1], rows), BF16)],
            [rec_hidden[0], gain],
            [],
        )
        across = xor_permute(blocks, "tp", 1)
        xs = [blocks, across, xor_permute(blocks, "sub", 1), xor_permute(across, "sub", 1)]
        from_d = line_pairs([(1, 2), (2, 1)])(from_a)
        from_c = line_pairs([(1, 0), (2, 3)])(from_b)
        over_a = across_groups(from_a, range(4))
        over_b = across_groups(from_b, (1, 2))
        from_e = line_pairs([(1, 0), (2, 3)])(from_d)
        over_c = across_groups(from_c, (0, 3))
        over_d = across_groups(from_d, (1, 2))
        over_e = across_groups(from_e, (0, 3))
        (acc,) = call(
            first_kernel,
            [shaped((tokens, 2 * width), F32)],
            [*xs, w_key, w_value, from_a, over_a, from_b, from_c, over_b, over_c],
            [],
            flops=3 * depth * tokens * width * 4,
        )
        far = [*xs, from_d, from_e, over_d, over_e]
    else:
        normed = lax.all_gather(
            normalize(rec_hidden[0], norm_gain), ("tp", "sub"), axis=0, tiled=True
        )
        acc = jnp.concatenate(
            [
                jnp.dot(
                    normed,
                    lax.all_gather(w, "rep", axis=0, tiled=True),
                    preferred_element_type=F32,
                )
                for w in (w_key, w_value)
            ],
            axis=1,
        )
        far = []

    lengths = seq_lengths[replica]
    arriving = (jnp.arange(seq_count) == listed_slot[replica]) & (replica >= half)
    moved_length = seq_lengths[partner, listed_slot[partner]]
    base = jnp.concatenate(
        [jnp.where(arriving, moved_length, lengths), jnp.full((1,), tokens, jnp.int32)]
    )
    positions = (base[:, None] + jnp.arange(steps, dtype=jnp.int32)[None, :]).reshape(-1)
    cosine, sine = rope_tables(positions, head_size)
    flat = (per, heads, head_size)
    num, den, moved, rows_last = call(
        functools.partial(attend_kernel, len(sums), seq_count, steps),
        [
            shaped(flat, F32),
            shaped(flat, F32),
            shaped((2, steps * heads, head_size), F32),
            shaped((steps * heads, width), BF16),
        ],
        [*sums, cosine, sine, qgain, kgain, pool_keys[0], pool_values[0]],
        [table, seq_lengths, listed_slot],
        scratch=[pltpu.VMEM(flat, F32)] * 3,
    )
    moved = lax.ppermute(moved, "rep", [(i, i + half) for i in range(half)])

    rec_k, rec_v, decoded = call(
        functools.partial(tail_kernel, bool(far), steps),
        [
            shaped((tokens, width), BF16),
            shaped((tokens, width), BF16),
            shaped((per, heads * head_size), BF16),
        ],
        [*far, acc, rec_cos, rec_sin, kgain, rows_last, num, den, moved],
        [listed_slot],
        scratch=[pltpu.VMEM(flat, F32)] + [pltpu.VMEM((tokens, 2 * width), F32)] * bool(far),
        flops=depth * tokens * width * 4,
    )
    return (rec_k[None], rec_v[None], decoded.reshape(1, slots, steps, heads * head_size))


def solution(mesh):
    in_specs = (
        P(("groups", "rep"), ("tp", "sub"), None),
        P(("groups", "rep"), None, None, None),
        P(),
        P(),
        P(),
        P("rep", ("tp", "sub")),
        P("rep", ("tp", "sub")),
        P("rep", ("tp", "sub")),
        P(("groups", "rep"), None, None, ("tp", "sub")),
        P(("groups", "rep"), None, None, ("tp", "sub")),
        P(("groups", "rep"), None, None),
        P("groups", None),
        P("groups"),
    )
    out_specs = (
        P(("groups", "rep"), None, ("tp", "sub")),
        P(("groups", "rep"), None, ("tp", "sub")),
        P(("groups", "rep"), None, None, ("tp", "sub")),
    )
    return jax.shard_map(body, mesh=mesh, in_specs=in_specs, out_specs=out_specs, check_vma=False)
```

```python
import functools
import math

import jax
import jax.numpy as jnp
import numpy as np
from jax import lax
from jax.experimental import pallas as pl
from jax.experimental.pallas import tpu as pltpu
from jax.sharding import PartitionSpec as P

EPSILON = 1e-06
ROPE_BASE = 1000000.0
KEEP_PAGES = 3
VMEM_BYTES = 16 * 2**20
F32 = jnp.float32
BF16 = jnp.bfloat16

WHOLE = pl.BlockSpec(memory_space=pltpu.VMEM)
SCALAR = pl.BlockSpec(memory_space=pltpu.SMEM)


def call(kernel, outs, ins, scalars, scratch=(), flops=0):
    bytes_accessed = sum(math.prod(a.shape) * a.dtype.itemsize for a in list(ins) + list(outs))
    return pl.pallas_call(
        kernel,
        out_shape=tuple(outs),
        in_specs=[SCALAR] * len(scalars) + [WHOLE] * len(ins),
        out_specs=tuple([WHOLE] * len(outs)),
        scratch_shapes=list(scratch),
        compiler_params=pltpu.CompilerParams(vmem_limit_bytes=VMEM_BYTES),
        cost_estimate=pl.CostEstimate(flops=flops, bytes_accessed=bytes_accessed, transcendentals=0),
    )(*scalars, *[pltpu.with_memory_space_constraint(a, pltpu.VMEM) for a in ins])


def shaped(shape, dtype):
    return jax.ShapeDtypeStruct(shape, dtype)


def dot(a, b):
    return jnp.dot(a, b, preferred_element_type=F32)


def dot_rows(a, b):
    return lax.dot_general(a, b, (((1,), (1,)), ((), ())), preferred_element_type=F32)


def xor_permute(value, axis, distance):
    count = lax.axis_size(axis)
    return lax.ppermute(value, axis, [(i, i ^ distance) for i in range(count)])


def head_scale(values):
    return lax.rsqrt(jnp.mean(values * values, axis=-1, keepdims=True) + EPSILON)


def rotate_rows(values, cosine, sine):
    return values * cosine + pltpu.roll(values, values.shape[-1] // 2, values.ndim - 1) * sine


def rope_freqs(head_size):
    half = np.arange(head_size // 2, dtype=np.float32)
    freqs = np.exp(half * np.float32(-2.0 * math.log(ROPE_BASE) / head_size)).astype(np.float32)
    return np.concatenate([freqs, freqs])[None]


def rope_tables(count, head_size):
    angles = np.arange(count, dtype=np.float32)[:, None] * rope_freqs(head_size)
    signs = np.where(np.arange(head_size) < head_size // 2, -1.0, 1.0)
    cosine, sine = np.cos(angles.astype(np.float64)), np.sin(angles.astype(np.float64)) * signs
    return jnp.asarray(cosine, F32), jnp.asarray(sine, F32)


def normalize(states, gain):
    values = states.astype(F32)
    return (values * head_scale(values) * gain).astype(BF16)


def norm_spread_kernel(x_ref, gain_ref, *outs):
    replica = lax.axis_index("rep")
    slots, steps, _ = x_ref.shape
    width = outs[0].shape[1]
    for slot in range(slots):
        values = x_ref[slot].astype(F32)
        scale = head_scale(values)
        for k, out in enumerate(outs):
            at = pl.multiple_of((replica ^ k) * width, 128)
            part = x_ref[slot, :, pl.ds(at, width)].astype(F32)
            out[slot * steps : (slot + 1) * steps, :] = (
                part * scale * gain_ref[:, pl.ds(at, width)]
            ).astype(BF16)


def project_kernel(count, steps, listed_ref, *refs):
    rows = refs[:count]
    wq_ref, wk_ref, wv_ref, own_ref = refs[count : count + 4]
    sent_refs, stacked = refs[count + 4 : -1], refs[-1]
    replica = lax.axis_index("rep")
    half = count // 2
    per = rows[0].shape[0]
    pad = stacked.shape[1]
    ids = lax.broadcasted_iota(jnp.int32, (per, 1), 0)
    for k in range(count):
        own = rows[k][...].astype(F32)
        other = rows[k ^ half][...].astype(F32)
        busy = (replica ^ k) < half
        for t in range(steps):
            from_row = ids == listed_ref[replica ^ k ^ half] * steps + t
            moved = jnp.sum(jnp.where(from_row, other, 0.0), axis=0, keepdims=True)
            own = jnp.where((ids == listed_ref[replica ^ k] * steps + t) & busy, moved, own)
        stacked[k, :per, :] = own.astype(BF16)
    lhs = stacked[...].reshape(-1, stacked.shape[2])
    width = wk_ref.shape[1]
    at = 0
    for w_ref, pieces in ((wq_ref, wq_ref.shape[1] // width), (wk_ref, 1), (wv_ref, 1)):
        for piece in range(pieces):
            product = dot(lhs, w_ref[:, piece * width : (piece + 1) * width])
            own_ref[:, at : at + width] = product[:per]
            for k in range(1, count):
                sent_refs[k - 1][:, at : at + width] = product[k * pad : k * pad + per].astype(BF16)
            at += width


def project_new(rows, listed, w_query, w_key, w_value, steps):
    count = len(rows)
    per, depth = rows[0].shape
    pad = -(-per // 16) * 16
    total = w_query.shape[1] + 2 * w_key.shape[1]
    return call(
        functools.partial(project_kernel, count, steps),
        [pltpu.VMEM((per, total), F32)] + [pltpu.VMEM((per, total), BF16)] * (count - 1),
        [*rows, w_query, w_key, w_value],
        [listed],
        scratch=[pltpu.VMEM((count, pad, depth), BF16)],
        flops=2 * count * per * depth * total,
    )


def spread_heads(rows, kv_heads):
    heads = kv_heads * 8
    ids = lax.broadcasted_iota(jnp.int32, (rows.shape[0], 1), 0) % heads // 8
    return jnp.concatenate([jnp.where(ids == k, rows, 0.0) for k in range(kv_heads)], axis=1)


def own_head(wide, kv_heads):
    size = wide.shape[1] // kv_heads
    heads = kv_heads * 8
    ids = lax.broadcasted_iota(jnp.int32, (wide.shape[0], 1), 0) % heads // 8
    total = wide[:, :size]
    for k in range(1, kv_heads):
        total = jnp.where(ids == k, wide[:, k * size : (k + 1) * size], total)
    return total


def attend_kernel(parts, seq_count, steps, tokens, table_ref, lengths_ref, listed_ref, *refs):
    sums = refs[:parts]
    freqs_ref, qgain_ref, kgain_ref, keys_ref, values_ref = refs[parts : parts + 5]
    num_ref, den_ref, moved_ref, last_ref, q3, k3, v3 = refs[parts + 5 :]
    replica = lax.axis_index("rep")
    half = lax.axis_size("rep") // 2
    size = qgain_ref.shape[1]
    width = keys_ref.shape[2]
    page = keys_ref.shape[1]
    kv_heads = width // size
    heads = kv_heads * 8
    slots = seq_count + 1
    per = slots * steps

    def total(at):
        value = sums[0][:, at : at + size].astype(F32)
        for other in sums[1:]:
            value = value + other[:, at : at + size].astype(F32)
        return value

    partner = jnp.where(replica < half, replica, replica - half)
    arrived = lengths_ref[partner, listed_ref[partner]]
    ids = lax.broadcasted_iota(jnp.int32, (per, 1), 0)
    positions = ids % steps
    for slot in range(slots):
        base = tokens
        if slot < seq_count:
            base = jnp.where(listed_ref[replica] == slot, arrived, lengths_ref[replica, slot])
        positions = positions + jnp.where(ids // steps == slot, base, 0)
    angles = positions.astype(F32) * freqs_ref[...]
    lanes = lax.broadcasted_iota(jnp.int32, (per, size), 1)
    cosine, sine = jnp.cos(angles), jnp.sin(angles)
    sine = jnp.where(lanes < size // 2, -sine, sine)

    for h in range(heads):
        x = total(h * size)
        x = rotate_rows(x * head_scale(x) * qgain_ref[...], cosine, sine) * size**-0.5
        q3[:, h, :] = x.astype(BF16).astype(F32)
    for h in range(kv_heads):
        x = total((heads + h) * size)
        x = rotate_rows(x * head_scale(x) * kgain_ref[...], cosine, sine).astype(BF16).astype(F32)
        k3[:, h * 8 : h * 8 + 8, :] = jnp.broadcast_to(x[:, None, :], (x.shape[0], 8, size))
        v = total((heads + kv_heads + h) * size).astype(BF16).astype(F32)
        v3[:, h * 8 : h * 8 + 8, :] = jnp.broadcast_to(v[:, None, :], (x.shape[0], 8, size))

    def old_terms(rows, page_of, length, pages, first):
        num, den = None, None
        for i in range(pages):
            at = first + i
            scores = dot_rows(rows, keys_ref[page_of(at)])
            ids = lax.broadcasted_iota(jnp.int32, scores.shape, 1) + at * page
            weights = jnp.where(ids < length, jnp.exp(scores), 0.0)
            part = jnp.sum(weights, axis=-1, keepdims=True)
            mixed = dot(weights.astype(BF16), values_ref[page_of(at)])
            num = mixed if num is None else num + mixed
            den = part if den is None else den + part
        return num, den

    def rows_of(slot):
        return q3[pl.ds(slot * steps, steps)].reshape(steps * heads, size)

    for slot in range(slots):
        q = q3[slot * steps : (slot + 1) * steps]
        k = k3[slot * steps : (slot + 1) * steps]
        v = v3[slot * steps : (slot + 1) * steps]
        nums, dens = [], []
        for t in range(steps):
            num, den = None, None
            for u in range(t + 1):
                e = jnp.exp(jnp.sum(q[t] * k[u], axis=-1, keepdims=True))
                num = e * v[u] if num is None else num + e * v[u]
                den = e if den is None else den + e
            nums.append(num)
            dens.append(den)
        num, den = jnp.concatenate(nums, axis=0), jnp.concatenate(dens, axis=0)
        rows = spread_heads(rows_of(slot), kv_heads).astype(BF16)
        if slot < seq_count:
            old_num, old_den = old_terms(
                rows, lambda at: table_ref[slot, at], lengths_ref[replica, slot], KEEP_PAGES, 0
            )
            num = num + own_head(old_num, kv_heads)
            den = den + old_den
        else:
            last_ref[...] = rows
        num_ref[slot * steps : (slot + 1) * steps] = num.reshape(steps, heads, size)
        den_ref[slot * steps : (slot + 1) * steps] = jnp.broadcast_to(den, num.shape).reshape(
            steps, heads, size
        )

    moved_ref[...] = jnp.zeros_like(moved_ref)

    @pl.when(replica < half)
    def _():
        slot = listed_ref[replica]
        length = lengths_ref[replica, slot]
        rows = spread_heads(rows_of(slot), kv_heads).astype(BF16)
        pages = table_ref.shape[1]
        at_once = 4

        def turn(i, carry):
            num, den = old_terms(rows, lambda at: table_ref[slot, at], length, at_once, i * at_once)
            return carry[0] + num, carry[1] + den

        num, den = lax.fori_loop(
            0,
            pages // at_once,
            turn,
            (jnp.zeros((steps * heads, width), F32), jnp.zeros((steps * heads, 1), F32)),
        )
        num = own_head(num, kv_heads)
        moved_ref[0] = num
        moved_ref[1] = jnp.broadcast_to(den, num.shape)


def norm_blocks_kernel(x_ref, gain_ref, out_ref):
    width = out_ref.shape[2]
    values = x_ref[...].astype(F32)
    scale = head_scale(values)
    for k, at in enumerate(half_blocks()):
        at = pl.multiple_of(at * width, 128)
        part = x_ref[:, pl.ds(at, width)].astype(F32)
        out_ref[k] = (part * scale * gain_ref[:, pl.ds(at, width)]).astype(BF16)


def half_blocks():
    replica, group = lax.axis_index("rep"), lax.axis_index("groups")
    second = jnp.where(replica < 2, 2, 1)
    third = jnp.where(replica < 2, 3, 0)
    order = [2 * replica, 2 * replica + 1]
    for source in (replica ^ 1, second, third):
        order += [2 * source + group, 2 * source + 1 - group]
    return order


def first_kernel(*refs):
    xs = refs[:4]
    wk_ref, wv_ref, a_ref, ya_ref, b_ref, c_ref, yb_ref, yc_ref, acc_ref = refs[4:]
    replica = lax.axis_index("rep")
    middle = (replica == 1) | (replica == 2)
    width = wk_ref.shape[1]
    depth = a_ref.shape[0]

    def block(k):
        return jnp.concatenate([x[k] for x in xs], axis=0)

    keys, values = None, None
    for k in range(2):
        x = block(k)
        more_k = dot(x, wk_ref[k * depth : (k + 1) * depth])
        more_v = dot(x, wv_ref[k * depth : (k + 1) * depth])
        keys = more_k if keys is None else keys + more_k
        values = more_v if values is None else values + more_v
    acc_ref[:, :width] = keys
    acc_ref[:, width:] = values
    acc_ref[...] += dot(block(2), a_ref[...])
    acc_ref[...] += dot(block(3), ya_ref[...])

    @pl.when(middle)
    def _():
        acc_ref[...] += dot(block(4), b_ref[...])
        acc_ref[...] += dot(block(5), yb_ref[...])

    @pl.when(jnp.logical_not(middle))
    def _():
        acc_ref[...] += dot(block(4), c_ref[...])
        acc_ref[...] += dot(block(5), yc_ref[...])


def tail_kernel(far, steps, listed_ref, *refs):
    if far:
        xs, (d_ref, e_ref, yd_ref, ye_ref) = refs[:4], refs[4:8]
        refs = refs[8:]
    acc_ref, cos_ref, sin_ref, kgain_ref, rows_ref, num_ref, den_ref, moved_ref = refs[:8]
    keys_ref, values_ref, out_ref, o3 = refs[8:12]
    replica = lax.axis_index("rep")
    half = lax.axis_size("rep") // 2
    tokens, width = keys_ref.shape
    size = kgain_ref.shape[1]
    kv_heads = width // size
    heads = kv_heads * 8
    slots = num_ref.shape[0] // steps

    if far:
        fresh = refs[12]
        middle = (replica == 1) | (replica == 2)

        def block(k):
            return jnp.concatenate([x[k] for x in xs], axis=0)

        @pl.when(middle)
        def _():
            fresh[...] = acc_ref[...] + dot(block(6), d_ref[...]) + dot(block(7), yd_ref[...])

        @pl.when(jnp.logical_not(middle))
        def _():
            fresh[...] = acc_ref[...] + dot(block(6), e_ref[...]) + dot(block(7), ye_ref[...])

        tp, sub = lax.axis_index("tp"), lax.axis_index("sub")
        places = [tp * 2 + sub, (tp ^ 1) * 2 + sub, tp * 2 + (sub ^ 1), (tp ^ 1) * 2 + (sub ^ 1)]
    else:
        fresh, places = acc_ref, [0]
    chunk = tokens // len(places)
    for i, place in enumerate(places):
        if len(places) > 1:
            place = pl.ds(pl.multiple_of(place * chunk, chunk), chunk)
        else:
            place = pl.ds(0, chunk)
        cosine, sine = cos_ref[place, :], sin_ref[place, :]
        for h in range(kv_heads):
            x = fresh[i * chunk : (i + 1) * chunk, h * size : (h + 1) * size]
            x = rotate_rows(x * head_scale(x) * kgain_ref[...], cosine, sine)
            keys_ref[place, h * size : (h + 1) * size] = x.astype(BF16)
        values_ref[place, :] = fresh[i * chunk : (i + 1) * chunk, width:].astype(BF16)

    weights = jnp.exp(dot_rows(rows_ref[...], keys_ref[...]))
    old_num = own_head(dot(weights.astype(BF16), values_ref[...]), kv_heads)
    old_den = jnp.sum(weights, axis=-1, keepdims=True)
    at = (slots - 1) * steps
    o3[:at] = num_ref[:at] / den_ref[:at]
    o3[at:] = (num_ref[at:] + old_num.reshape(steps, heads, size)) / (
        den_ref[at:] + jnp.broadcast_to(old_den, old_num.shape).reshape(steps, heads, size)
    )
    mine = pl.ds(listed_ref[replica] * steps, steps)
    live = jnp.where(replica < half, 0.0, 1.0)
    o3[mine] = (
        live
        * (num_ref[mine] + moved_ref[0].reshape(steps, heads, size))
        / (den_ref[mine] + moved_ref[1].reshape(steps, heads, size))
    )
    for h in range(heads):
        for slot in range(slots):
            out_ref[slot, :, h * size : (h + 1) * size] = o3[
                slot * steps : (slot + 1) * steps, h, :
            ].astype(BF16)


def line_pairs(pairs, axis="rep"):
    return lambda value: lax.ppermute(value, axis, pairs)


def across_groups(value, replicas):
    count = lax.axis_size("rep")
    pairs = [(g * count + r, (1 - g) * count + r) for g in range(2) for r in replicas]
    return lax.ppermute(value, ("groups", "rep"), pairs)


def body(
    rec_hidden,
    dec_hidden,
    norm_gain,
    query_gain,
    key_gain,
    w_query,
    w_key,
    w_value,
    pool_keys,
    pool_values,
    page_table,
    seq_lengths,
    listed_slot,
):
    replicas = lax.axis_size("rep")
    half = replicas // 2
    replica = lax.axis_index("rep")
    head_size = query_gain.shape[0]
    width = w_key.shape[1]
    depth = w_key.shape[0]
    _, slots, steps, features = dec_hidden.shape
    seq_count = slots - 1
    per = slots * steps
    heads = w_query.shape[1] // head_size
    gain = norm_gain[None]
    qgain, kgain = query_gain[None], key_gain[None]
    table = page_table[0]
    tokens = rec_hidden.shape[1] * lax.axis_size("tp") * lax.axis_size("sub")
    near = (
        replicas == 4
        and lax.axis_size("tp") == 2
        and lax.axis_size("sub") == 2
        and lax.axis_size("groups") == 2
    )

    if near:
        group = lax.axis_index("groups")
        rows = depth // 2
        own = jnp.concatenate(
            [lax.dynamic_slice_in_dim(w, group * rows, rows, 0) for w in (w_key, w_value)], axis=1
        )

    if near:
        spread = call(
            norm_spread_kernel, [pltpu.VMEM((per, depth), BF16)] * replicas, [dec_hidden[0], gain], []
        )
        rec_hidden, *spread = lax.optimization_barrier((rec_hidden, *spread))
        (blocks,) = call(
            norm_blocks_kernel,
            [pltpu.VMEM((2 * replicas, rec_hidden.shape[1], rows), BF16)],
            [rec_hidden[0], gain],
            [],
        )
        spread = [spread[0]] + [xor_permute(spread[k], "rep", k) for k in range(1, replicas)]
        own, *spread = lax.optimization_barrier((own, *spread))
        from_a = line_pairs([(0, 1), (1, 0), (2, 3), (3, 2)])(own)
        from_b = line_pairs([(1, 2), (2, 1)])(own)
        own_sums, *sent = project_new(spread, listed_slot, w_query, w_key, w_value, steps)
        sums = [xor_permute(sent[k - 1], "rep", k) for k in range(1, replicas)]
        from_a, from_b, _ = lax.optimization_barrier((from_a, from_b, sent[0]))
        late_a, blocks, *sums = lax.optimization_barrier((from_a, blocks, *sums))
        sums = [own_sums, *sums]
    else:
        spread = lax.all_to_all(
            normalize(dec_hidden[0].reshape(per, features), norm_gain), "rep", split_axis=1, concat_axis=0, tiled=True
        ).reshape(replicas, slots, steps, depth)
        moved = jnp.take_along_axis(spread, listed_slot[:, None, None, None], axis=1)
        moved = jnp.roll(moved, half, axis=0)
        ids = jnp.arange(replicas)[:, None]
        swap = (jnp.arange(slots)[None] == listed_slot[:, None]) & (ids < half)
        spread = jnp.where(swap[:, :, None, None], moved, spread).reshape(replicas * per, depth)
        weights = jnp.concatenate([w_query, w_key, w_value], axis=1)
        sums = [
            lax.psum_scatter(
                jnp.dot(spread, weights, preferred_element_type=F32),
                "rep",
                scatter_dimension=0,
                tiled=True,
            )
        ]

    rec_cos, rec_sin = rope_tables(tokens, head_size)
    if near:
        across = xor_permute(blocks, "tp", 1)
        from_d = line_pairs([(1, 2), (2, 1)])(from_a)
        from_c = line_pairs([(1, 0), (2, 3)])(from_b)
        over_a = across_groups(late_a, range(4))
    else:
        normed = lax.all_gather(
            normalize(rec_hidden[0], norm_gain), ("tp", "sub"), axis=0, tiled=True
        )
        acc = jnp.concatenate(
            [
                jnp.dot(
                    normed,
                    lax.all_gather(w, "rep", axis=0, tiled=True),
                    preferred_element_type=F32,
                )
                for w in (w_key, w_value)
            ],
            axis=1,
        )

    flat = (per, heads, head_size)
    num, den, moved, rows_last = call(
        functools.partial(attend_kernel, len(sums), seq_count, steps, tokens),
        [
            pltpu.VMEM(flat, F32),
            pltpu.VMEM(flat, F32),
            pltpu.VMEM((2, steps * heads, head_size), F32),
            pltpu.VMEM((steps * heads, width), BF16),
        ],
        [*sums, jnp.asarray(rope_freqs(head_size)), qgain, kgain, pool_keys[0], pool_values[0]],
        [table, seq_lengths, listed_slot],
        scratch=[pltpu.VMEM(flat, F32)] * 3,
    )
    far = []
    if near:
        from_b, from_c, from_d, num, den, moved, rows_last = lax.optimization_barrier(
            (from_b, from_c, from_d, num, den, moved, rows_last)
        )
        from_e = line_pairs([(1, 0), (2, 3)])(from_d)
        over_b = across_groups(from_b, (1, 2))
        over_c = across_groups(from_c, (0, 3))
        beside = xor_permute(blocks, "sub", 1)
        across, beside, from_d, from_e, over_a, over_b, over_c, moved = lax.optimization_barrier(
            (across, beside, from_d, from_e, over_a, over_b, over_c, moved)
        )
        over_d = across_groups(from_d, (1, 2))
        over_e = across_groups(from_e, (0, 3))
        xs = [blocks, across, beside, xor_permute(across, "sub", 1)]
        (acc,) = call(
            first_kernel,
            [pltpu.VMEM((tokens, 2 * width), F32)],
            [*xs, w_key, w_value, from_a, over_a, from_b, from_c, over_b, over_c],
            [],
            flops=3 * depth * tokens * width * 4,
        )
        far = [*xs, from_d, from_e, over_d, over_e]
    moved = lax.ppermute(moved, "rep", [(i, i + half) for i in range(half)])

    rec_k, rec_v, decoded = call(
        functools.partial(tail_kernel, bool(far), steps),
        [
            shaped((tokens, width), BF16),
            shaped((tokens, width), BF16),
            shaped((slots, steps, heads * head_size), BF16),
        ],
        [*far, acc, rec_cos, rec_sin, kgain, rows_last, num, den, moved],
        [listed_slot],
        scratch=[pltpu.VMEM(flat, F32)] + [pltpu.VMEM((tokens, 2 * width), F32)] * bool(far),
        flops=depth * tokens * width * 4,
    )
    return (rec_k[None], rec_v[None], decoded[None])


def solution(mesh):
    in_specs = (
        P(("groups", "rep"), ("tp", "sub"), None),
        P(("groups", "rep"), None, None, None),
        P(),
        P(),
        P(),
        P("rep", ("tp", "sub")),
        P("rep", ("tp", "sub")),
        P("rep", ("tp", "sub")),
        P(("groups", "rep"), None, None, ("tp", "sub")),
        P(("groups", "rep"), None, None, ("tp", "sub")),
        P(("groups", "rep"), None, None),
        P("groups", None),
        P("groups"),
    )
    out_specs = (
        P(("groups", "rep"), None, ("tp", "sub")),
        P(("groups", "rep"), None, ("tp", "sub")),
        P(("groups", "rep"), None, None, ("tp", "sub")),
    )
    return jax.shard_map(body, mesh=mesh, in_specs=in_specs, out_specs=out_specs, check_vma=False)
```

```python
import functools
import math

import jax
import jax.numpy as jnp
import numpy as np
from jax import lax
from jax.experimental import pallas as pl
from jax.experimental.pallas import tpu as pltpu
from jax.sharding import PartitionSpec as P

EPSILON = 1e-06
ROPE_BASE = 1000000.0
KEEP_PAGES = 3
VMEM_BYTES = 16 * 2**20
F32 = jnp.float32
BF16 = jnp.bfloat16

WHOLE = pl.BlockSpec(memory_space=pltpu.VMEM)
SCALAR = pl.BlockSpec(memory_space=pltpu.SMEM)


def call(kernel, outs, ins, scalars, scratch=(), flops=0):
    bytes_accessed = sum(math.prod(a.shape) * a.dtype.itemsize for a in list(ins) + list(outs))
    return pl.pallas_call(
        kernel,
        out_shape=tuple(outs),
        in_specs=[SCALAR] * len(scalars) + [WHOLE] * len(ins),
        out_specs=tuple([WHOLE] * len(outs)),
        scratch_shapes=list(scratch),
        compiler_params=pltpu.CompilerParams(vmem_limit_bytes=VMEM_BYTES),
        cost_estimate=pl.CostEstimate(flops=flops, bytes_accessed=bytes_accessed, transcendentals=0),
    )(*scalars, *[pltpu.with_memory_space_constraint(a, pltpu.VMEM) for a in ins])


def shaped(shape, dtype):
    return jax.ShapeDtypeStruct(shape, dtype)


def dot(a, b):
    return jnp.dot(a, b, preferred_element_type=F32)


def dot_rows(a, b):
    return lax.dot_general(a, b, (((1,), (1,)), ((), ())), preferred_element_type=F32)


def xor_permute(value, axis, distance):
    count = lax.axis_size(axis)
    return lax.ppermute(value, axis, [(i, i ^ distance) for i in range(count)])


def head_scale(values):
    return lax.rsqrt(jnp.mean(values * values, axis=-1, keepdims=True) + EPSILON)


def rotate_rows(values, cosine, sine):
    return values * cosine + pltpu.roll(values, values.shape[-1] // 2, values.ndim - 1) * sine


def rope_freqs(head_size):
    half = np.arange(head_size // 2, dtype=np.float32)
    freqs = np.exp(half * np.float32(-2.0 * math.log(ROPE_BASE) / head_size)).astype(np.float32)
    return np.concatenate([freqs, freqs])[None]


def rope_tables(count, head_size):
    angles = np.arange(count, dtype=np.float32)[:, None] * rope_freqs(head_size)
    signs = np.where(np.arange(head_size) < head_size // 2, -1.0, 1.0)
    cosine, sine = np.cos(angles.astype(np.float64)), np.sin(angles.astype(np.float64)) * signs
    return jnp.asarray(cosine, F32), jnp.asarray(sine, F32)


def normalize(states, gain):
    values = states.astype(F32)
    return (values * head_scale(values) * gain).astype(BF16)


def norm_spread_kernel(x_ref, gain_ref, *outs):
    replica = lax.axis_index("rep")
    slots, steps, _ = x_ref.shape
    width = outs[0].shape[1]
    for slot in range(slots):
        values = x_ref[slot].astype(F32)
        scale = head_scale(values)
        for k, out in enumerate(outs):
            at = pl.multiple_of((replica ^ k) * width, 128)
            part = x_ref[slot, :, pl.ds(at, width)].astype(F32)
            out[slot * steps : (slot + 1) * steps, :] = (
                part * scale * gain_ref[:, pl.ds(at, width)]
            ).astype(BF16)


def project_kernel(count, steps, listed_ref, *refs):
    rows = refs[:count]
    wq_ref, wk_ref, wv_ref, own_ref = refs[count : count + 4]
    pair_ref, far_ref, stacked = refs[count + 4 :]
    replica = lax.axis_index("rep")
    half = count // 2
    per = rows[0].shape[0]
    pad = stacked.shape[1]
    ids = lax.broadcasted_iota(jnp.int32, (per, 1), 0)
    for k in range(count):
        own = rows[k][...].astype(F32)
        other = rows[k ^ half][...].astype(F32)
        busy = (replica ^ k) < half
        for t in range(steps):
            from_row = ids == listed_ref[replica ^ k ^ half] * steps + t
            moved = jnp.sum(jnp.where(from_row, other, 0.0), axis=0, keepdims=True)
            own = jnp.where((ids == listed_ref[replica ^ k] * steps + t) & busy, moved, own)
        stacked[k, :per, :] = own.astype(BF16)
    lhs = stacked[...].reshape(-1, stacked.shape[2])
    width = wk_ref.shape[1]
    at = 0
    for w_ref, pieces in ((wq_ref, wq_ref.shape[1] // width), (wk_ref, 1), (wv_ref, 1)):
        for piece in range(pieces):
            product = dot(lhs, w_ref[:, piece * width : (piece + 1) * width])
            own_ref[:, at : at + width] = product[:per]
            for i, k in enumerate((1, 3)):
                pair_ref[i, :, at : at + width] = product[k * pad : k * pad + per].astype(BF16)
            far_ref[:, at : at + width] = product[2 * pad : 2 * pad + per]
            at += width


def project_new(rows, listed, w_query, w_key, w_value, steps):
    count = len(rows)
    per, depth = rows[0].shape
    pad = -(-per // 16) * 16
    total = w_query.shape[1] + 2 * w_key.shape[1]
    return call(
        functools.partial(project_kernel, count, steps),
        [
            pltpu.VMEM((per, total), F32),
            pltpu.VMEM((2, per, total), BF16),
            pltpu.VMEM((per, total), F32),
        ],
        [*rows, w_query, w_key, w_value],
        [listed],
        scratch=[pltpu.VMEM((count, pad, depth), BF16)],
        flops=2 * count * per * depth * total,
    )


def spread_heads(rows, kv_heads):
    heads = kv_heads * 8
    ids = lax.broadcasted_iota(jnp.int32, (rows.shape[0], 1), 0) % heads // 8
    return jnp.concatenate([jnp.where(ids == k, rows, 0.0) for k in range(kv_heads)], axis=1)


def own_head(wide, kv_heads):
    size = wide.shape[1] // kv_heads
    heads = kv_heads * 8
    ids = lax.broadcasted_iota(jnp.int32, (wide.shape[0], 1), 0) % heads // 8
    total = wide[:, :size]
    for k in range(1, kv_heads):
        total = jnp.where(ids == k, wide[:, k * size : (k + 1) * size], total)
    return total


def old_terms(rows, keys_ref, values_ref, page_of, length, pages, first):
    page = keys_ref.shape[1]
    num, den = None, None
    for i in range(pages):
        at = first + i
        scores = dot_rows(rows, keys_ref[page_of(at)])
        ids = lax.broadcasted_iota(jnp.int32, scores.shape, 1) + at * page
        weights = jnp.where(ids < length, jnp.exp(scores), 0.0)
        part = jnp.sum(weights, axis=-1, keepdims=True)
        mixed = dot(weights.astype(BF16), values_ref[page_of(at)])
        num = mixed if num is None else num + mixed
        den = part if den is None else den + part
    return num, den


def queries_kernel(parts, seq_count, steps, tokens, table_ref, lengths_ref, listed_ref, *refs):
    sums = refs[:parts]
    freqs_ref, qgain_ref, kgain_ref, keys_ref, values_ref = refs[parts : parts + 5]
    q3, k3, v3, moved_ref = refs[parts + 5 :]
    replica = lax.axis_index("rep")
    half = lax.axis_size("rep") // 2
    size = qgain_ref.shape[1]
    width = keys_ref.shape[2]
    kv_heads = width // size
    heads = kv_heads * 8
    slots = seq_count + 1
    per = slots * steps

    def total(at):
        value = sums[0][:, at : at + size].astype(F32)
        for other in sums[1:]:
            part = other[0] if len(other.shape) == 3 else other[...]
            value = value + part[:, at : at + size].astype(F32)
        return value

    partner = jnp.where(replica < half, replica, replica - half)
    arrived = lengths_ref[partner, listed_ref[partner]]
    ids = lax.broadcasted_iota(jnp.int32, (per, 1), 0)
    positions = ids % steps
    for slot in range(slots):
        base = tokens
        if slot < seq_count:
            base = jnp.where(listed_ref[replica] == slot, arrived, lengths_ref[replica, slot])
        positions = positions + jnp.where(ids // steps == slot, base, 0)
    angles = positions.astype(F32) * freqs_ref[...]
    lanes = lax.broadcasted_iota(jnp.int32, (per, size), 1)
    cosine, sine = jnp.cos(angles), jnp.sin(angles)
    sine = jnp.where(lanes < size // 2, -sine, sine)

    for h in range(heads):
        x = total(h * size)
        x = rotate_rows(x * head_scale(x) * qgain_ref[...], cosine, sine) * size**-0.5
        q3[:, h, :] = x.astype(BF16).astype(F32)
    for h in range(kv_heads):
        x = total((heads + h) * size)
        x = rotate_rows(x * head_scale(x) * kgain_ref[...], cosine, sine).astype(BF16).astype(F32)
        k3[:, h * 8 : h * 8 + 8, :] = jnp.broadcast_to(x[:, None, :], (per, 8, size))
        v = total((heads + kv_heads + h) * size).astype(BF16).astype(F32)
        v3[:, h * 8 : h * 8 + 8, :] = jnp.broadcast_to(v[:, None, :], (per, 8, size))

    moved_ref[...] = jnp.zeros_like(moved_ref)

    @pl.when(replica < half)
    def _():
        slot = listed_ref[replica]
        length = lengths_ref[replica, slot]
        rows = q3[pl.ds(slot * steps, steps)].reshape(steps * heads, size)
        rows = spread_heads(rows, kv_heads).astype(BF16)
        num, den = old_terms(
            rows, keys_ref, values_ref, lambda at: table_ref[slot, at], length, table_ref.shape[1], 0
        )
        num = own_head(num, kv_heads)
        moved_ref[0] = num
        moved_ref[1] = jnp.broadcast_to(den, num.shape)


def attend_kernel(seq_count, steps, table_ref, lengths_ref, *refs):
    q3, k3, v3, keys_ref, values_ref, num_ref, den_ref, last_ref = refs
    replica = lax.axis_index("rep")
    heads, size = q3.shape[1:]
    kv_heads = keys_ref.shape[2] // size
    for slot in range(seq_count + 1):
        q = q3[slot * steps : (slot + 1) * steps]
        k = k3[slot * steps : (slot + 1) * steps]
        v = v3[slot * steps : (slot + 1) * steps]
        nums, dens = [], []
        for t in range(steps):
            num, den = None, None
            for u in range(t + 1):
                e = jnp.exp(jnp.sum(q[t] * k[u], axis=-1, keepdims=True))
                num = e * v[u] if num is None else num + e * v[u]
                den = e if den is None else den + e
            nums.append(num)
            dens.append(den)
        num, den = jnp.concatenate(nums, axis=0), jnp.concatenate(dens, axis=0)
        rows = spread_heads(q.reshape(steps * heads, size), kv_heads).astype(BF16)
        if slot < seq_count:
            old_num, old_den = old_terms(
                rows,
                keys_ref,
                values_ref,
                lambda at: table_ref[slot, at],
                lengths_ref[replica, slot],
                KEEP_PAGES,
                0,
            )
            num = num + own_head(old_num, kv_heads)
            den = den + old_den
        else:
            last_ref[...] = rows
        num_ref[slot * steps : (slot + 1) * steps] = num.reshape(steps, heads, size)
        den_ref[slot * steps : (slot + 1) * steps] = jnp.broadcast_to(den, num.shape).reshape(
            steps, heads, size
        )


def norm_blocks_kernel(x_ref, gain_ref, out_ref):
    width = out_ref.shape[2]
    values = x_ref[...].astype(F32)
    scale = head_scale(values)
    for k, at in enumerate(half_blocks()):
        at = pl.multiple_of(at * width, 128)
        part = x_ref[:, pl.ds(at, width)].astype(F32)
        out_ref[k] = (part * scale * gain_ref[:, pl.ds(at, width)]).astype(BF16)


def half_blocks():
    replica, group = lax.axis_index("rep"), lax.axis_index("groups")
    second = jnp.where(replica < 2, 2, 1)
    third = jnp.where(replica < 2, 3, 0)
    order = [2 * replica, 2 * replica + 1]
    for source in (replica ^ 1, second, third):
        order += [2 * source + group, 2 * source + 1 - group]
    return order


def first_kernel(*refs):
    xs, (wk_ref, wv_ref), (a_ref, ya_ref, b_ref, c_ref, yb_ref, yc_ref) = refs[:4], refs[4:6], refs[6:12]
    acc_ref = refs[12]
    replica = lax.axis_index("rep")
    middle = (replica == 1) | (replica == 2)
    width = wk_ref.shape[1]
    depth = a_ref.shape[0]

    def block(k):
        return jnp.concatenate([x[k] for x in xs], axis=0)

    keys, values = None, None
    for k in range(2):
        more_k = dot(block(k), wk_ref[k * depth : (k + 1) * depth])
        more_v = dot(block(k), wv_ref[k * depth : (k + 1) * depth])
        keys = more_k if keys is None else keys + more_k
        values = more_v if values is None else values + more_v
    both = dot(block(2), a_ref[...]) + dot(block(3), ya_ref[...])
    acc_ref[:, :width] = keys + both[:, :width]
    acc_ref[:, width:] = values + both[:, width:]

    @pl.when(middle)
    def _():
        acc_ref[...] += dot(block(4), b_ref[...]) + dot(block(5), yb_ref[...])

    @pl.when(jnp.logical_not(middle))
    def _():
        acc_ref[...] += dot(block(4), c_ref[...]) + dot(block(5), yc_ref[...])


def tail_kernel(far, steps, listed_ref, *refs):
    if far:
        xs, (d_ref, yd_ref, ek_ref, ev_ref, yek_ref, yev_ref) = refs[:4], refs[4:10]
        refs = refs[10:]
    acc_ref, cos_ref, sin_ref, kgain_ref, rows_ref, num_ref, den_ref, moved_ref = refs[:8]
    keys_ref, values_ref, out_ref, o3 = refs[8:12]
    replica = lax.axis_index("rep")
    half = lax.axis_size("rep") // 2
    tokens, width = keys_ref.shape
    size = kgain_ref.shape[1]
    kv_heads = width // size
    heads = kv_heads * 8
    slots = num_ref.shape[0] // steps

    if far:
        fresh = refs[12]
        middle = (replica == 1) | (replica == 2)

        def block(k):
            return jnp.concatenate([x[k] for x in xs], axis=0)

        @pl.when(middle)
        def _():
            fresh[...] = acc_ref[...] + dot(block(6), d_ref[...]) + dot(block(7), yd_ref[...])

        @pl.when(jnp.logical_not(middle))
        def _():
            fresh[...] = acc_ref[...] + dot(block(6), ek_ref[...]) + dot(block(7), yek_ref[...])

        tp, sub = lax.axis_index("tp"), lax.axis_index("sub")
        places = [tp * 2 + sub, (tp ^ 1) * 2 + sub, tp * 2 + (sub ^ 1), (tp ^ 1) * 2 + (sub ^ 1)]
    else:
        fresh, places = acc_ref, [0]
    chunk = tokens // len(places)
    for i, place in enumerate(places):
        if len(places) > 1:
            place = pl.ds(pl.multiple_of(place * chunk, chunk), chunk)
        else:
            place = pl.ds(0, chunk)
        cosine, sine = cos_ref[place, :], sin_ref[place, :]
        for h in range(kv_heads):
            x = fresh[i * chunk : (i + 1) * chunk, h * size : (h + 1) * size]
            x = rotate_rows(x * head_scale(x) * kgain_ref[...], cosine, sine)
            keys_ref[place, h * size : (h + 1) * size] = x.astype(BF16)
        values_ref[place, :] = fresh[i * chunk : (i + 1) * chunk, width:].astype(BF16)

    weights = jnp.exp(dot_rows(rows_ref[...], keys_ref[...]))
    old_num = own_head(dot(weights.astype(BF16), values_ref[...]), kv_heads)
    old_den = jnp.sum(weights, axis=-1, keepdims=True)
    at = (slots - 1) * steps
    o3[:at] = num_ref[:at] / den_ref[:at]
    o3[at:] = (num_ref[at:] + old_num.reshape(steps, heads, size)) / (
        den_ref[at:] + jnp.broadcast_to(old_den, old_num.shape).reshape(steps, heads, size)
    )
    mine = pl.ds(listed_ref[replica] * steps, steps)
    live = jnp.where(replica < half, 0.0, 1.0)
    o3[mine] = (
        live
        * (num_ref[mine] + moved_ref[0].reshape(steps, heads, size))
        / (den_ref[mine] + moved_ref[1].reshape(steps, heads, size))
    )
    for h in range(heads):
        for slot in range(slots):
            out_ref[slot, :, h * size : (h + 1) * size] = o3[
                slot * steps : (slot + 1) * steps, h, :
            ].astype(BF16)


def after(value, *others):
    return lax.optimization_barrier((value, *others))[0]


def line_pairs(pairs, axis="rep"):
    return lambda value: lax.ppermute(value, axis, pairs)


def across_groups(value, replicas):
    count = lax.axis_size("rep")
    pairs = [(g * count + r, (1 - g) * count + r) for g in range(2) for r in replicas]
    return lax.ppermute(value, ("groups", "rep"), pairs)


def diagonal(value, pairs):
    count = lax.axis_size("rep")
    pairs = [(count * g + a, count * (1 - g) + b) for g in range(2) for a, b in pairs]
    return lax.ppermute(value, ("groups", "rep"), pairs)


def body(
    rec_hidden,
    dec_hidden,
    norm_gain,
    query_gain,
    key_gain,
    w_query,
    w_key,
    w_value,
    pool_keys,
    pool_values,
    page_table,
    seq_lengths,
    listed_slot,
):
    replicas = lax.axis_size("rep")
    half = replicas // 2
    replica = lax.axis_index("rep")
    head_size = query_gain.shape[0]
    width = w_key.shape[1]
    depth = w_key.shape[0]
    _, slots, steps, features = dec_hidden.shape
    seq_count = slots - 1
    per = slots * steps
    heads = w_query.shape[1] // head_size
    gain = norm_gain[None]
    qgain, kgain = query_gain[None], key_gain[None]
    table = page_table[0]
    tokens = rec_hidden.shape[1] * lax.axis_size("tp") * lax.axis_size("sub")
    near = (
        replicas == 4
        and lax.axis_size("tp") == 2
        and lax.axis_size("sub") == 2
        and lax.axis_size("groups") == 2
    )

    rec_cos, rec_sin = rope_tables(tokens, head_size)
    flat = (per, heads, head_size)
    keys, values = pool_keys[0], pool_values[0]

    def queries(*sums):
        return call(
            functools.partial(queries_kernel, len(sums), seq_count, steps, tokens),
            [pltpu.VMEM(flat, F32)] * 3 + [pltpu.VMEM((2, steps * heads, head_size), F32)],
            [*sums, jnp.asarray(rope_freqs(head_size)), qgain, kgain, keys, values],
            [table, seq_lengths, listed_slot],
        )

    def attend(q3, k3, v3):
        return call(
            functools.partial(attend_kernel, seq_count, steps),
            [pltpu.VMEM(flat, F32)] * 2 + [pltpu.VMEM((steps * heads, width), BF16)],
            [q3, k3, v3, keys, values],
            [table, seq_lengths],
        )

    if near:
        group = lax.axis_index("groups")
        middle = (replica == 1) | (replica == 2)
        rows = depth // 2
        own = jnp.concatenate(
            [lax.dynamic_slice_in_dim(w, group * rows, rows, 0) for w in (w_key, w_value)], axis=1
        )
        spread = call(
            norm_spread_kernel, [pltpu.VMEM((per, depth), BF16)] * 4, [dec_hidden[0], gain], []
        )
        (blocks,) = call(
            norm_blocks_kernel,
            [pltpu.VMEM((2 * replicas, rec_hidden.shape[1], rows), BF16)],
            [rec_hidden[0], gain],
            [],
        )
        s1 = xor_permute(spread[1], "rep", 1)
        s2 = xor_permute(spread[2], "rep", 2)
        s3 = xor_permute(spread[3], "rep", 3)
        from_a = line_pairs([(0, 1), (1, 0), (2, 3), (3, 2)])(after(own, s1, s2, s3))
        from_b = line_pairs([(1, 2), (2, 1)])(after(own, s1, s2, s3))
        across = xor_permute(after(blocks, s1, s2, s3), "tp", 1)
        own_sums, pair, far_sums = project_new(
            [spread[0], s1, s2, s3], listed_slot, w_query, w_key, w_value, steps
        )
        from_d = line_pairs([(1, 2), (2, 1)])(after(from_a, from_b, far_sums))
        from_c = line_pairs([(1, 0), (2, 3)])(after(from_b, from_a, far_sums))
        beside = xor_permute(after(blocks, from_d, from_c), "sub", 1)
        over_c = across_groups(from_c, (0, 3))
        pair_in = xor_permute(pair, "rep", 1)
        over_a = across_groups(after(from_a, pair_in), range(4))
        over_b = across_groups(after(from_b, pair_in), (1, 2))
        r2 = xor_permute((far_sums + pair_in[1].astype(F32)).astype(BF16), "rep", 2)
        from_e = line_pairs([(1, 0), (2, 3)])(after(from_d, from_c, r2))
        over_e = across_groups(after(from_e, across, over_a, over_b, over_c), (0, 3))
        over_d = across_groups(after(from_d, from_e, over_a, over_b, over_c), (1, 2))
        corner = xor_permute(after(across, from_e, over_a, over_b, over_c), "sub", 1)
        (acc,) = call(
            first_kernel,
            [pltpu.VMEM((tokens, 2 * width), F32)],
            [blocks, across, beside, corner, w_key, w_value, from_a, over_a, from_b, from_c, over_b, over_c],
            [],
            flops=3 * depth * tokens * width * 4,
        )
        q3, k3, v3, moved = queries(own_sums, pair_in, r2)
        returned = lax.ppermute(after(moved, from_e), "rep", [(i, i + half) for i in range(half)])
        num, den, rows_last = attend(q3, k3, v3)
        far = [blocks, across, beside, corner, from_d, over_d, from_e, from_e, over_e, over_e]
    else:
        spread = lax.all_to_all(
            normalize(dec_hidden[0].reshape(per, features), norm_gain), "rep", split_axis=1, concat_axis=0, tiled=True
        ).reshape(replicas, slots, steps, depth)
        moved = jnp.take_along_axis(spread, listed_slot[:, None, None, None], axis=1)
        moved = jnp.roll(moved, half, axis=0)
        ids = jnp.arange(replicas)[:, None]
        swap = (jnp.arange(slots)[None] == listed_slot[:, None]) & (ids < half)
        spread = jnp.where(swap[:, :, None, None], moved, spread).reshape(replicas * per, depth)
        weights = jnp.concatenate([w_query, w_key, w_value], axis=1)
        sums = [
            lax.psum_scatter(
                jnp.dot(spread, weights, preferred_element_type=F32),
                "rep",
                scatter_dimension=0,
                tiled=True,
            )
        ]
        normed = lax.all_gather(
            normalize(rec_hidden[0], norm_gain), ("tp", "sub"), axis=0, tiled=True
        )
        acc = jnp.concatenate(
            [
                jnp.dot(
                    normed,
                    lax.all_gather(w, "rep", axis=0, tiled=True),
                    preferred_element_type=F32,
                )
                for w in (w_key, w_value)
            ],
            axis=1,
        )
        far = []
        q3, k3, v3, moved = queries(*sums)
        returned = lax.ppermute(moved, "rep", [(i, i + half) for i in range(half)])
        num, den, rows_last = attend(q3, k3, v3)

    rec_k, rec_v, decoded = call(
        functools.partial(tail_kernel, bool(far), steps),
        [
            shaped((tokens, width), BF16),
            shaped((tokens, width), BF16),
            shaped((slots, steps, heads * head_size), BF16),
        ],
        [*far, acc, rec_cos, rec_sin, kgain, rows_last, num, den, returned],
        [listed_slot],
        scratch=[pltpu.VMEM(flat, F32)] + [pltpu.VMEM((tokens, 2 * width), F32)] * bool(far),
        flops=depth * tokens * width * 4,
    )
    return (rec_k[None], rec_v[None], decoded[None])


def solution(mesh):
    in_specs = (
        P(("groups", "rep"), ("tp", "sub"), None),
        P(("groups", "rep"), None, None, None),
        P(),
        P(),
        P(),
        P("rep", ("tp", "sub")),
        P("rep", ("tp", "sub")),
        P("rep", ("tp", "sub")),
        P(("groups", "rep"), None, None, ("tp", "sub")),
        P(("groups", "rep"), None, None, ("tp", "sub")),
        P(("groups", "rep"), None, None),
        P("groups", None),
        P("groups"),
    )
    out_specs = (
        P(("groups", "rep"), None, ("tp", "sub")),
        P(("groups", "rep"), None, ("tp", "sub")),
        P(("groups", "rep"), None, None, ("tp", "sub")),
    )
    return jax.shard_map(body, mesh=mesh, in_specs=in_specs, out_specs=out_specs, check_vma=False)
```

```python
import functools
import math

import jax
import jax.numpy as jnp
import numpy as np
from jax import lax
from jax.experimental import pallas as pl
from jax.experimental.pallas import tpu as pltpu
from jax.sharding import PartitionSpec as P

EPSILON = 1e-06
ROPE_BASE = 1000000.0
KEEP_PAGES = 3
VMEM_BYTES = 16 * 2**20
F32 = jnp.float32
BF16 = jnp.bfloat16

WHOLE = pl.BlockSpec(memory_space=pltpu.VMEM)
SCALAR = pl.BlockSpec(memory_space=pltpu.SMEM)


def call(kernel, outs, ins, scalars, scratch=(), flops=0):
    bytes_accessed = sum(math.prod(a.shape) * a.dtype.itemsize for a in list(ins) + list(outs))
    return pl.pallas_call(
        kernel,
        out_shape=tuple(outs),
        in_specs=[SCALAR] * len(scalars) + [WHOLE] * len(ins),
        out_specs=tuple([WHOLE] * len(outs)),
        scratch_shapes=list(scratch),
        compiler_params=pltpu.CompilerParams(vmem_limit_bytes=VMEM_BYTES),
        cost_estimate=pl.CostEstimate(flops=flops, bytes_accessed=bytes_accessed, transcendentals=0),
    )(*scalars, *[pltpu.with_memory_space_constraint(a, pltpu.VMEM) for a in ins])


def shaped(shape, dtype):
    return jax.ShapeDtypeStruct(shape, dtype)


def dot(a, b):
    return jnp.dot(a, b, preferred_element_type=F32)


def dot_rows(a, b):
    return lax.dot_general(a, b, (((1,), (1,)), ((), ())), preferred_element_type=F32)


def xor_permute(value, axis, distance):
    count = lax.axis_size(axis)
    return lax.ppermute(value, axis, [(i, i ^ distance) for i in range(count)])


def head_scale(values):
    return lax.rsqrt(jnp.mean(values * values, axis=-1, keepdims=True) + EPSILON)


def rotate_rows(values, cosine, sine):
    return values * cosine + pltpu.roll(values, values.shape[-1] // 2, values.ndim - 1) * sine


def rope_freqs(head_size):
    half = np.arange(head_size // 2, dtype=np.float32)
    freqs = np.exp(half * np.float32(-2.0 * math.log(ROPE_BASE) / head_size)).astype(np.float32)
    return np.concatenate([freqs, freqs])[None]


def rope_tables(count, head_size):
    angles = np.arange(count, dtype=np.float32)[:, None] * rope_freqs(head_size)
    signs = np.where(np.arange(head_size) < head_size // 2, -1.0, 1.0)
    cosine, sine = np.cos(angles.astype(np.float64)), np.sin(angles.astype(np.float64)) * signs
    return jnp.asarray(cosine, F32), jnp.asarray(sine, F32)


def normalize(states, gain):
    values = states.astype(F32)
    return (values * head_scale(values) * gain).astype(BF16)


def norm_spread_kernel(x_ref, gain_ref, *outs):
    replica = lax.axis_index("rep")
    slots, steps, _ = x_ref.shape
    width = outs[0].shape[1]
    for slot in range(slots):
        values = x_ref[slot].astype(F32)
        scale = head_scale(values)
        for k, out in enumerate(outs):
            at = pl.multiple_of((replica ^ k) * width, 128)
            part = x_ref[slot, :, pl.ds(at, width)].astype(F32)
            out[slot * steps : (slot + 1) * steps, :] = (
                part * scale * gain_ref[:, pl.ds(at, width)]
            ).astype(BF16)


def project_kernel(count, steps, listed_ref, *refs):
    rows = refs[:count]
    wq_ref, wk_ref, wv_ref, own_ref = refs[count : count + 4]
    pair_ref, far_ref, stacked = refs[count + 4 :]
    replica = lax.axis_index("rep")
    half = count // 2
    per = rows[0].shape[0]
    pad = stacked.shape[1]
    ids = lax.broadcasted_iota(jnp.int32, (per, 1), 0)
    for k in range(count):
        own = rows[k][...].astype(F32)
        other = rows[k ^ half][...].astype(F32)
        busy = (replica ^ k) < half
        for t in range(steps):
            from_row = ids == listed_ref[replica ^ k ^ half] * steps + t
            moved = jnp.sum(jnp.where(from_row, other, 0.0), axis=0, keepdims=True)
            own = jnp.where((ids == listed_ref[replica ^ k] * steps + t) & busy, moved, own)
        stacked[k, :per, :] = own.astype(BF16)
    lhs = stacked[...].reshape(-1, stacked.shape[2])
    width = wk_ref.shape[1]
    at = 0
    for w_ref, pieces in ((wq_ref, wq_ref.shape[1] // width), (wk_ref, 1), (wv_ref, 1)):
        for piece in range(pieces):
            product = dot(lhs, w_ref[:, piece * width : (piece + 1) * width])
            own_ref[:, at : at + width] = product[:per]
            for i, k in enumerate((1, 3)):
                pair_ref[i, :, at : at + width] = product[k * pad : k * pad + per].astype(BF16)
            far_ref[:, at : at + width] = product[2 * pad : 2 * pad + per]
            at += width


def project_new(rows, listed, w_query, w_key, w_value, steps):
    count = len(rows)
    per, depth = rows[0].shape
    pad = -(-per // 16) * 16
    total = w_query.shape[1] + 2 * w_key.shape[1]
    return call(
        functools.partial(project_kernel, count, steps),
        [
            pltpu.VMEM((per, total), F32),
            pltpu.VMEM((2, per, total), BF16),
            pltpu.VMEM((per, total), F32),
        ],
        [*rows, w_query, w_key, w_value],
        [listed],
        scratch=[pltpu.VMEM((count, pad, depth), BF16)],
        flops=2 * count * per * depth * total,
    )


def spread_heads(rows, kv_heads):
    heads = kv_heads * 8
    ids = lax.broadcasted_iota(jnp.int32, (rows.shape[0], 1), 0) % heads // 8
    return jnp.concatenate([jnp.where(ids == k, rows, 0.0) for k in range(kv_heads)], axis=1)


def own_head(wide, kv_heads):
    size = wide.shape[1] // kv_heads
    heads = kv_heads * 8
    ids = lax.broadcasted_iota(jnp.int32, (wide.shape[0], 1), 0) % heads // 8
    total = wide[:, :size]
    for k in range(1, kv_heads):
        total = jnp.where(ids == k, wide[:, k * size : (k + 1) * size], total)
    return total


def old_terms(rows, keys_ref, values_ref, page_of, length, pages, first):
    page = keys_ref.shape[1]
    num, den = None, None
    for i in range(pages):
        at = first + i
        scores = dot_rows(rows, keys_ref[page_of(at)])
        ids = lax.broadcasted_iota(jnp.int32, scores.shape, 1) + at * page
        weights = jnp.where(ids < length, jnp.exp(scores), 0.0)
        part = jnp.sum(weights, axis=-1, keepdims=True)
        mixed = dot(weights.astype(BF16), values_ref[page_of(at)])
        num = mixed if num is None else num + mixed
        den = part if den is None else den + part
    return num, den


def queries_kernel(parts, seq_count, steps, tokens, table_ref, lengths_ref, listed_ref, *refs):
    sums = refs[:parts]
    freqs_ref, qgain_ref, kgain_ref, keys_ref, values_ref = refs[parts : parts + 5]
    q3, k3, v3, moved_ref = refs[parts + 5 :]
    replica = lax.axis_index("rep")
    half = lax.axis_size("rep") // 2
    size = qgain_ref.shape[1]
    width = keys_ref.shape[2]
    kv_heads = width // size
    heads = kv_heads * 8
    slots = seq_count + 1
    per = slots * steps

    def total(at):
        value = sums[0][:, at : at + size].astype(F32)
        for other in sums[1:]:
            part = other[0] if len(other.shape) == 3 else other[...]
            value = value + part[:, at : at + size].astype(F32)
        return value

    partner = jnp.where(replica < half, replica, replica - half)
    arrived = lengths_ref[partner, listed_ref[partner]]
    ids = lax.broadcasted_iota(jnp.int32, (per, 1), 0)
    positions = ids % steps
    for slot in range(slots):
        base = tokens
        if slot < seq_count:
            base = jnp.where(listed_ref[replica] == slot, arrived, lengths_ref[replica, slot])
        positions = positions + jnp.where(ids // steps == slot, base, 0)
    angles = positions.astype(F32) * freqs_ref[...]
    lanes = lax.broadcasted_iota(jnp.int32, (per, size), 1)
    cosine, sine = jnp.cos(angles), jnp.sin(angles)
    sine = jnp.where(lanes < size // 2, -sine, sine)

    for h in range(heads):
        x = total(h * size)
        x = rotate_rows(x * head_scale(x) * qgain_ref[...], cosine, sine) * size**-0.5
        q3[:, h, :] = x.astype(BF16).astype(F32)
    for h in range(kv_heads):
        x = total((heads + h) * size)
        x = rotate_rows(x * head_scale(x) * kgain_ref[...], cosine, sine).astype(BF16).astype(F32)
        k3[:, h * 8 : h * 8 + 8, :] = jnp.broadcast_to(x[:, None, :], (per, 8, size))
        v = total((heads + kv_heads + h) * size).astype(BF16).astype(F32)
        v3[:, h * 8 : h * 8 + 8, :] = jnp.broadcast_to(v[:, None, :], (per, 8, size))

    moved_ref[...] = jnp.zeros_like(moved_ref)

    @pl.when(replica < half)
    def _():
        slot = listed_ref[replica]
        length = lengths_ref[replica, slot]
        rows = q3[pl.ds(slot * steps, steps)].reshape(steps * heads, size)
        rows = spread_heads(rows, kv_heads).astype(BF16)
        num, den = old_terms(
            rows, keys_ref, values_ref, lambda at: table_ref[slot, at], length, table_ref.shape[1], 0
        )
        num = own_head(num, kv_heads)
        moved_ref[0] = num
        moved_ref[1] = jnp.broadcast_to(den, num.shape)


def attend_kernel(seq_count, steps, table_ref, lengths_ref, *refs):
    q3, k3, v3, keys_ref, values_ref, num_ref, den_ref, last_ref = refs
    replica = lax.axis_index("rep")
    heads, size = q3.shape[1:]
    kv_heads = keys_ref.shape[2] // size
    for slot in range(seq_count + 1):
        q = q3[slot * steps : (slot + 1) * steps]
        k = k3[slot * steps : (slot + 1) * steps]
        v = v3[slot * steps : (slot + 1) * steps]
        nums, dens = [], []
        for t in range(steps):
            num, den = None, None
            for u in range(t + 1):
                e = jnp.exp(jnp.sum(q[t] * k[u], axis=-1, keepdims=True))
                num = e * v[u] if num is None else num + e * v[u]
                den = e if den is None else den + e
            nums.append(num)
            dens.append(den)
        num, den = jnp.concatenate(nums, axis=0), jnp.concatenate(dens, axis=0)
        rows = spread_heads(q.reshape(steps * heads, size), kv_heads).astype(BF16)
        if slot < seq_count:
            old_num, old_den = old_terms(
                rows,
                keys_ref,
                values_ref,
                lambda at: table_ref[slot, at],
                lengths_ref[replica, slot],
                KEEP_PAGES,
                0,
            )
            num = num + own_head(old_num, kv_heads)
            den = den + old_den
        else:
            last_ref[...] = rows
        num_ref[slot * steps : (slot + 1) * steps] = num.reshape(steps, heads, size)
        den_ref[slot * steps : (slot + 1) * steps] = jnp.broadcast_to(den, num.shape).reshape(
            steps, heads, size
        )


def norm_blocks_kernel(x_ref, gain_ref, out_ref):
    width = out_ref.shape[2]
    values = x_ref[...].astype(F32)
    scale = head_scale(values)
    for k, at in enumerate(half_blocks()):
        at = pl.multiple_of(at * width, 128)
        part = x_ref[:, pl.ds(at, width)].astype(F32)
        out_ref[k] = (part * scale * gain_ref[:, pl.ds(at, width)]).astype(BF16)


def half_blocks():
    replica, group = lax.axis_index("rep"), lax.axis_index("groups")
    second = jnp.where(replica < 2, 2, 1)
    third = jnp.where(replica < 2, 3, 0)
    order = [2 * replica, 2 * replica + 1]
    for source in (replica ^ 1, second, third):
        order += [2 * source + group, 2 * source + 1 - group]
    return order


def first_kernel(*refs):
    xs, (wk_ref, wv_ref), (a_ref, ya_ref, b_ref, c_ref, yb_ref, yc_ref) = refs[:4], refs[4:6], refs[6:12]
    acc_ref = refs[12]
    replica = lax.axis_index("rep")
    middle = (replica == 1) | (replica == 2)
    width = wk_ref.shape[1]
    depth = a_ref.shape[0]

    def block(k):
        return jnp.concatenate([x[k] for x in xs], axis=0)

    keys, values = None, None
    for k in range(2):
        more_k = dot(block(k), wk_ref[k * depth : (k + 1) * depth])
        more_v = dot(block(k), wv_ref[k * depth : (k + 1) * depth])
        keys = more_k if keys is None else keys + more_k
        values = more_v if values is None else values + more_v
    both = dot(block(2), a_ref[...]) + dot(block(3), ya_ref[...])
    acc_ref[:, :width] = keys + both[:, :width]
    acc_ref[:, width:] = values + both[:, width:]

    @pl.when(middle)
    def _():
        acc_ref[...] += dot(block(4), b_ref[...]) + dot(block(5), yb_ref[...])

    @pl.when(jnp.logical_not(middle))
    def _():
        acc_ref[...] += dot(block(4), c_ref[...]) + dot(block(5), yc_ref[...])


def tail_kernel(far, steps, listed_ref, *refs):
    if far:
        xs, (d_ref, yd_ref, ek_ref, ev_ref, yek_ref, yev_ref) = refs[:4], refs[4:10]
        refs = refs[10:]
    acc_ref, cos_ref, sin_ref, kgain_ref, rows_ref, num_ref, den_ref, moved_ref = refs[:8]
    keys_ref, values_ref, out_ref, o3 = refs[8:12]
    replica = lax.axis_index("rep")
    half = lax.axis_size("rep") // 2
    tokens, width = keys_ref.shape
    size = kgain_ref.shape[1]
    kv_heads = width // size
    heads = kv_heads * 8
    slots = num_ref.shape[0] // steps

    if far:
        fresh = refs[12]
        middle = (replica == 1) | (replica == 2)

        def block(k):
            return jnp.concatenate([x[k] for x in xs], axis=0)

        @pl.when(middle)
        def _():
            fresh[...] = acc_ref[...] + dot(block(6), d_ref[...]) + dot(block(7), yd_ref[...])

        @pl.when(jnp.logical_not(middle))
        def _():
            fresh[...] = acc_ref[...] + dot(block(6), ek_ref[...]) + dot(block(7), yek_ref[...])

        tp, sub = lax.axis_index("tp"), lax.axis_index("sub")
        places = [tp * 2 + sub, (tp ^ 1) * 2 + sub, tp * 2 + (sub ^ 1), (tp ^ 1) * 2 + (sub ^ 1)]
    else:
        fresh, places = acc_ref, [0]
    chunk = tokens // len(places)
    for i, place in enumerate(places):
        if len(places) > 1:
            place = pl.ds(pl.multiple_of(place * chunk, chunk), chunk)
        else:
            place = pl.ds(0, chunk)
        cosine, sine = cos_ref[place, :], sin_ref[place, :]
        for h in range(kv_heads):
            x = fresh[i * chunk : (i + 1) * chunk, h * size : (h + 1) * size]
            x = rotate_rows(x * head_scale(x) * kgain_ref[...], cosine, sine)
            keys_ref[place, h * size : (h + 1) * size] = x.astype(BF16)
        values_ref[place, :] = fresh[i * chunk : (i + 1) * chunk, width:].astype(BF16)

    weights = jnp.exp(dot_rows(rows_ref[...], keys_ref[...]))
    old_num = own_head(dot(weights.astype(BF16), values_ref[...]), kv_heads)
    old_den = jnp.sum(weights, axis=-1, keepdims=True)
    at = (slots - 1) * steps
    o3[:at] = num_ref[:at] / den_ref[:at]
    o3[at:] = (num_ref[at:] + old_num.reshape(steps, heads, size)) / (
        den_ref[at:] + jnp.broadcast_to(old_den, old_num.shape).reshape(steps, heads, size)
    )
    mine = pl.ds(listed_ref[replica] * steps, steps)
    live = jnp.where(replica < half, 0.0, 1.0)
    o3[mine] = (
        live
        * (num_ref[mine] + moved_ref[0].reshape(steps, heads, size))
        / (den_ref[mine] + moved_ref[1].reshape(steps, heads, size))
    )
    for h in range(heads):
        for slot in range(slots):
            out_ref[slot, :, h * size : (h + 1) * size] = o3[
                slot * steps : (slot + 1) * steps, h, :
            ].astype(BF16)


def after(value, *others):
    return lax.optimization_barrier((value, *others))[0]


def line_pairs(pairs, axis="rep"):
    return lambda value: lax.ppermute(value, axis, pairs)


def across_groups(value, replicas):
    count = lax.axis_size("rep")
    pairs = [(g * count + r, (1 - g) * count + r) for g in range(2) for r in replicas]
    return lax.ppermute(value, ("groups", "rep"), pairs)


def diagonal(value, pairs):
    count = lax.axis_size("rep")
    pairs = [(count * g + a, count * (1 - g) + b) for g in range(2) for a, b in pairs]
    return lax.ppermute(value, ("groups", "rep"), pairs)


def body(
    rec_hidden,
    dec_hidden,
    norm_gain,
    query_gain,
    key_gain,
    w_query,
    w_key,
    w_value,
    pool_keys,
    pool_values,
    page_table,
    seq_lengths,
    listed_slot,
):
    replicas = lax.axis_size("rep")
    half = replicas // 2
    replica = lax.axis_index("rep")
    head_size = query_gain.shape[0]
    width = w_key.shape[1]
    depth = w_key.shape[0]
    _, slots, steps, features = dec_hidden.shape
    seq_count = slots - 1
    per = slots * steps
    heads = w_query.shape[1] // head_size
    gain = norm_gain[None]
    qgain, kgain = query_gain[None], key_gain[None]
    table = page_table[0]
    tokens = rec_hidden.shape[1] * lax.axis_size("tp") * lax.axis_size("sub")
    near = (
        replicas == 4
        and lax.axis_size("tp") == 2
        and lax.axis_size("sub") == 2
        and lax.axis_size("groups") == 2
    )

    rec_cos, rec_sin = rope_tables(tokens, head_size)
    flat = (per, heads, head_size)
    keys, values = pool_keys[0], pool_values[0]

    def queries(*sums):
        return call(
            functools.partial(queries_kernel, len(sums), seq_count, steps, tokens),
            [pltpu.VMEM(flat, F32)] * 3 + [pltpu.VMEM((2, steps * heads, head_size), F32)],
            [*sums, jnp.asarray(rope_freqs(head_size)), qgain, kgain, keys, values],
            [table, seq_lengths, listed_slot],
        )

    def attend(q3, k3, v3):
        return call(
            functools.partial(attend_kernel, seq_count, steps),
            [pltpu.VMEM(flat, F32)] * 2 + [pltpu.VMEM((steps * heads, width), BF16)],
            [q3, k3, v3, keys, values],
            [table, seq_lengths],
        )

    if near:
        group = lax.axis_index("groups")
        middle = (replica == 1) | (replica == 2)
        rows = depth // 2
        own = jnp.concatenate(
            [lax.dynamic_slice_in_dim(w, group * rows, rows, 0) for w in (w_key, w_value)], axis=1
        )
        spread = call(
            norm_spread_kernel, [pltpu.VMEM((per, depth), BF16)] * 4, [dec_hidden[0], gain], []
        )
        (blocks,) = call(
            norm_blocks_kernel,
            [pltpu.VMEM((2 * replicas, rec_hidden.shape[1], rows), BF16)],
            [rec_hidden[0], gain],
            [],
        )
        s1 = xor_permute(spread[1], "rep", 1)
        s2 = xor_permute(spread[2], "rep", 2)
        s3 = xor_permute(spread[3], "rep", 3)
        from_a = line_pairs([(0, 1), (1, 0), (2, 3), (3, 2)])(own)
        from_b = line_pairs([(1, 2), (2, 1)])(own)
        across = xor_permute(after(blocks, s1, s2, s3), "tp", 1)
        own_sums, pair, far_sums = project_new(
            [spread[0], s1, s2, s3], listed_slot, w_query, w_key, w_value, steps
        )
        from_d = line_pairs([(1, 2), (2, 1)])(after(from_a, from_b))
        from_c = line_pairs([(1, 0), (2, 3)])(after(from_b, from_a))
        beside = xor_permute(after(blocks, from_d, from_c), "sub", 1)
        over_a = across_groups(after(from_a, s1, s2, s3), range(4))
        over_b = across_groups(after(from_b, from_d, from_c), (1, 2))
        over_c = across_groups(from_c, (0, 3))
        pair_in = xor_permute(pair, "rep", 1)
        r2 = xor_permute((far_sums + pair_in[1].astype(F32)).astype(BF16), "rep", 2)
        from_e = line_pairs([(1, 0), (2, 3)])(after(from_d, from_c, pair_in))
        over_e = across_groups(after(from_e, across, over_a, over_b, over_c), (0, 3))
        over_d = across_groups(after(from_d, from_e, over_a, over_b, over_c), (1, 2))
        corner = xor_permute(after(across, from_e, over_a, over_b, over_c), "sub", 1)
        (acc,) = call(
            first_kernel,
            [pltpu.VMEM((tokens, 2 * width), F32)],
            [blocks, across, beside, corner, w_key, w_value, from_a, over_a, from_b, from_c, over_b, over_c],
            [],
            flops=3 * depth * tokens * width * 4,
        )
        q3, k3, v3, moved = queries(after(own_sums, acc), pair_in, r2)
        returned = lax.ppermute(moved, "rep", [(i, i + half) for i in range(half)])
        num, den, rows_last = attend(q3, k3, v3)
        far = [blocks, across, beside, corner, from_d, over_d, from_e, from_e, over_e, over_e]
    else:
        spread = lax.all_to_all(
            normalize(dec_hidden[0].reshape(per, features), norm_gain), "rep", split_axis=1, concat_axis=0, tiled=True
        ).reshape(replicas, slots, steps, depth)
        moved = jnp.take_along_axis(spread, listed_slot[:, None, None, None], axis=1)
        moved = jnp.roll(moved, half, axis=0)
        ids = jnp.arange(replicas)[:, None]
        swap = (jnp.arange(slots)[None] == listed_slot[:, None]) & (ids < half)
        spread = jnp.where(swap[:, :, None, None], moved, spread).reshape(replicas * per, depth)
        weights = jnp.concatenate([w_query, w_key, w_value], axis=1)
        sums = [
            lax.psum_scatter(
                jnp.dot(spread, weights, preferred_element_type=F32),
                "rep",
                scatter_dimension=0,
                tiled=True,
            )
        ]
        normed = lax.all_gather(
            normalize(rec_hidden[0], norm_gain), ("tp", "sub"), axis=0, tiled=True
        )
        acc = jnp.concatenate(
            [
                jnp.dot(
                    normed,
                    lax.all_gather(w, "rep", axis=0, tiled=True),
                    preferred_element_type=F32,
                )
                for w in (w_key, w_value)
            ],
            axis=1,
        )
        far = []
        q3, k3, v3, moved = queries(*sums)
        returned = lax.ppermute(moved, "rep", [(i, i + half) for i in range(half)])
        num, den, rows_last = attend(q3, k3, v3)

    rec_k, rec_v, decoded = call(
        functools.partial(tail_kernel, bool(far), steps),
        [
            shaped((tokens, width), BF16),
            shaped((tokens, width), BF16),
            shaped((slots, steps, heads * head_size), BF16),
        ],
        [*far, acc, rec_cos, rec_sin, kgain, rows_last, num, den, returned],
        [listed_slot],
        scratch=[pltpu.VMEM(flat, F32)] + [pltpu.VMEM((tokens, 2 * width), F32)] * bool(far),
        flops=depth * tokens * width * 4,
    )
    return (rec_k[None], rec_v[None], decoded[None])


def solution(mesh):
    in_specs = (
        P(("groups", "rep"), ("tp", "sub"), None),
        P(("groups", "rep"), None, None, None),
        P(),
        P(),
        P(),
        P("rep", ("tp", "sub")),
        P("rep", ("tp", "sub")),
        P("rep", ("tp", "sub")),
        P(("groups", "rep"), None, None, ("tp", "sub")),
        P(("groups", "rep"), None, None, ("tp", "sub")),
        P(("groups", "rep"), None, None),
        P("groups", None),
        P("groups"),
    )
    out_specs = (
        P(("groups", "rep"), None, ("tp", "sub")),
        P(("groups", "rep"), None, ("tp", "sub")),
        P(("groups", "rep"), None, None, ("tp", "sub")),
    )
    return jax.shard_map(body, mesh=mesh, in_specs=in_specs, out_specs=out_specs, check_vma=False)
```

```python
import functools
import math

import jax
import jax.numpy as jnp
import numpy as np
from jax import lax
from jax.experimental import pallas as pl
from jax.experimental.pallas import tpu as pltpu
from jax.sharding import PartitionSpec as P

EPSILON = 1e-06
ROPE_BASE = 1000000.0
KEEP_PAGES = 3
VMEM_BYTES = 16 * 2**20
F32 = jnp.float32
BF16 = jnp.bfloat16

WHOLE = pl.BlockSpec(memory_space=pltpu.VMEM)
SCALAR = pl.BlockSpec(memory_space=pltpu.SMEM)


def call(kernel, outs, ins, scalars, scratch=(), flops=0):
    bytes_accessed = sum(math.prod(a.shape) * a.dtype.itemsize for a in list(ins) + list(outs))
    return pl.pallas_call(
        kernel,
        out_shape=tuple(outs),
        in_specs=[SCALAR] * len(scalars) + [WHOLE] * len(ins),
        out_specs=tuple([WHOLE] * len(outs)),
        scratch_shapes=list(scratch),
        compiler_params=pltpu.CompilerParams(vmem_limit_bytes=VMEM_BYTES),
        cost_estimate=pl.CostEstimate(flops=flops, bytes_accessed=bytes_accessed, transcendentals=0),
    )(*scalars, *[pltpu.with_memory_space_constraint(a, pltpu.VMEM) for a in ins])


def shaped(shape, dtype):
    return jax.ShapeDtypeStruct(shape, dtype)


def dot(a, b):
    return jnp.dot(a, b, preferred_element_type=F32)


def dot_rows(a, b):
    return lax.dot_general(a, b, (((1,), (1,)), ((), ())), preferred_element_type=F32)


def xor_permute(value, axis, distance):
    count = lax.axis_size(axis)
    return lax.ppermute(value, axis, [(i, i ^ distance) for i in range(count)])


def head_scale(values):
    return lax.rsqrt(jnp.mean(values * values, axis=-1, keepdims=True) + EPSILON)


def rotate_rows(values, cosine, sine):
    return values * cosine + pltpu.roll(values, values.shape[-1] // 2, values.ndim - 1) * sine


def rope_freqs(head_size):
    half = np.arange(head_size // 2, dtype=np.float32)
    freqs = np.exp(half * np.float32(-2.0 * math.log(ROPE_BASE) / head_size)).astype(np.float32)
    return np.concatenate([freqs, freqs])[None]


def rope_tables(count, head_size):
    angles = np.arange(count, dtype=np.float32)[:, None] * rope_freqs(head_size)
    signs = np.where(np.arange(head_size) < head_size // 2, -1.0, 1.0)
    cosine, sine = np.cos(angles.astype(np.float64)), np.sin(angles.astype(np.float64)) * signs
    return jnp.asarray(cosine, F32), jnp.asarray(sine, F32)


def normalize(states, gain):
    values = states.astype(F32)
    return (values * head_scale(values) * gain).astype(BF16)


def norm_spread_kernel(x_ref, gain_ref, *outs):
    replica = lax.axis_index("rep")
    slots, steps, _ = x_ref.shape
    width = outs[0].shape[1]
    for slot in range(slots):
        values = x_ref[slot].astype(F32)
        scale = head_scale(values)
        for k, out in enumerate(outs):
            at = pl.multiple_of((replica ^ k) * width, 128)
            part = x_ref[slot, :, pl.ds(at, width)].astype(F32)
            out[slot * steps : (slot + 1) * steps, :] = (
                part * scale * gain_ref[:, pl.ds(at, width)]
            ).astype(BF16)


def project_kernel(count, steps, listed_ref, *refs):
    rows = refs[:count]
    wq_ref, wk_ref, wv_ref, own_ref = refs[count : count + 4]
    pair_ref, far_ref, stacked = refs[count + 4 :]
    replica = lax.axis_index("rep")
    half = count // 2
    per = rows[0].shape[0]
    pad = stacked.shape[1]
    ids = lax.broadcasted_iota(jnp.int32, (per, 1), 0)
    for k in range(count):
        own = rows[k][...].astype(F32)
        other = rows[k ^ half][...].astype(F32)
        busy = (replica ^ k) < half
        for t in range(steps):
            from_row = ids == listed_ref[replica ^ k ^ half] * steps + t
            moved = jnp.sum(jnp.where(from_row, other, 0.0), axis=0, keepdims=True)
            own = jnp.where((ids == listed_ref[replica ^ k] * steps + t) & busy, moved, own)
        stacked[k, :per, :] = own.astype(BF16)
    lhs = stacked[...].reshape(-1, stacked.shape[2])
    width = wk_ref.shape[1]
    at = 0
    for w_ref, pieces in ((wq_ref, wq_ref.shape[1] // width), (wk_ref, 1), (wv_ref, 1)):
        for piece in range(pieces):
            product = dot(lhs, w_ref[:, piece * width : (piece + 1) * width])
            own_ref[:, at : at + width] = product[:per]
            for i, k in enumerate((1, 3)):
                pair_ref[i, :, at : at + width] = product[k * pad : k * pad + per].astype(BF16)
            far_ref[:, at : at + width] = product[2 * pad : 2 * pad + per]
            at += width


def project_new(rows, listed, w_query, w_key, w_value, steps):
    count = len(rows)
    per, depth = rows[0].shape
    pad = -(-per // 16) * 16
    total = w_query.shape[1] + 2 * w_key.shape[1]
    return call(
        functools.partial(project_kernel, count, steps),
        [
            pltpu.VMEM((per, total), F32),
            pltpu.VMEM((2, per, total), BF16),
            pltpu.VMEM((per, total), F32),
        ],
        [*rows, w_query, w_key, w_value],
        [listed],
        scratch=[pltpu.VMEM((count, pad, depth), BF16)],
        flops=2 * count * per * depth * total,
    )


def spread_heads(rows, kv_heads):
    heads = kv_heads * 8
    ids = lax.broadcasted_iota(jnp.int32, (rows.shape[0], 1), 0) % heads // 8
    return jnp.concatenate([jnp.where(ids == k, rows, 0.0) for k in range(kv_heads)], axis=1)


def own_head(wide, kv_heads):
    size = wide.shape[1] // kv_heads
    heads = kv_heads * 8
    ids = lax.broadcasted_iota(jnp.int32, (wide.shape[0], 1), 0) % heads // 8
    total = wide[:, :size]
    for k in range(1, kv_heads):
        total = jnp.where(ids == k, wide[:, k * size : (k + 1) * size], total)
    return total


def old_terms(rows, keys_ref, values_ref, page_of, length, pages, first):
    page = keys_ref.shape[1]
    num, den = None, None
    for i in range(pages):
        at = first + i
        scores = dot_rows(rows, keys_ref[page_of(at)])
        ids = lax.broadcasted_iota(jnp.int32, scores.shape, 1) + at * page
        weights = jnp.where(ids < length, jnp.exp(scores), 0.0)
        part = jnp.sum(weights, axis=-1, keepdims=True)
        mixed = dot(weights.astype(BF16), values_ref[page_of(at)])
        num = mixed if num is None else num + mixed
        den = part if den is None else den + part
    return num, den


def queries_kernel(parts, seq_count, steps, tokens, table_ref, lengths_ref, listed_ref, *refs):
    sums = refs[:parts]
    freqs_ref, qgain_ref, kgain_ref, keys_ref, values_ref = refs[parts : parts + 5]
    q3, k3, v3, moved_ref = refs[parts + 5 :]
    replica = lax.axis_index("rep")
    half = lax.axis_size("rep") // 2
    size = qgain_ref.shape[1]
    width = keys_ref.shape[2]
    kv_heads = width // size
    heads = kv_heads * 8
    slots = seq_count + 1
    per = slots * steps

    def total(at):
        value = sums[0][:, at : at + size].astype(F32)
        for other in sums[1:]:
            part = other[0] if len(other.shape) == 3 else other[...]
            value = value + part[:, at : at + size].astype(F32)
        return value

    partner = jnp.where(replica < half, replica, replica - half)
    arrived = lengths_ref[partner, listed_ref[partner]]
    ids = lax.broadcasted_iota(jnp.int32, (per, 1), 0)
    positions = ids % steps
    for slot in range(slots):
        base = tokens
        if slot < seq_count:
            base = jnp.where(listed_ref[replica] == slot, arrived, lengths_ref[replica, slot])
        positions = positions + jnp.where(ids // steps == slot, base, 0)
    angles = positions.astype(F32) * freqs_ref[...]
    lanes = lax.broadcasted_iota(jnp.int32, (per, size), 1)
    cosine, sine = jnp.cos(angles), jnp.sin(angles)
    sine = jnp.where(lanes < size // 2, -sine, sine)

    for h in range(heads):
        x = total(h * size)
        x = rotate_rows(x * head_scale(x) * qgain_ref[...], cosine, sine) * size**-0.5
        q3[:, h, :] = x.astype(BF16).astype(F32)
    for h in range(kv_heads):
        x = total((heads + h) * size)
        x = rotate_rows(x * head_scale(x) * kgain_ref[...], cosine, sine).astype(BF16).astype(F32)
        k3[:, h * 8 : h * 8 + 8, :] = jnp.broadcast_to(x[:, None, :], (per, 8, size))
        v = total((heads + kv_heads + h) * size).astype(BF16).astype(F32)
        v3[:, h * 8 : h * 8 + 8, :] = jnp.broadcast_to(v[:, None, :], (per, 8, size))

    moved_ref[...] = jnp.zeros_like(moved_ref)

    @pl.when(replica < half)
    def _():
        slot = listed_ref[replica]
        length = lengths_ref[replica, slot]
        rows = q3[pl.ds(slot * steps, steps)].reshape(steps * heads, size)
        rows = spread_heads(rows, kv_heads).astype(BF16)
        num, den = old_terms(
            rows, keys_ref, values_ref, lambda at: table_ref[slot, at], length, table_ref.shape[1], 0
        )
        num = own_head(num, kv_heads)
        moved_ref[0] = num
        moved_ref[1] = jnp.broadcast_to(den, num.shape)


def attend_kernel(seq_count, steps, table_ref, lengths_ref, *refs):
    q3, k3, v3, keys_ref, values_ref, num_ref, den_ref, last_ref = refs
    replica = lax.axis_index("rep")
    heads, size = q3.shape[1:]
    kv_heads = keys_ref.shape[2] // size
    for slot in range(seq_count + 1):
        q = q3[slot * steps : (slot + 1) * steps]
        k = k3[slot * steps : (slot + 1) * steps]
        v = v3[slot * steps : (slot + 1) * steps]
        nums, dens = [], []
        for t in range(steps):
            num, den = None, None
            for u in range(t + 1):
                e = jnp.exp(jnp.sum(q[t] * k[u], axis=-1, keepdims=True))
                num = e * v[u] if num is None else num + e * v[u]
                den = e if den is None else den + e
            nums.append(num)
            dens.append(den)
        num, den = jnp.concatenate(nums, axis=0), jnp.concatenate(dens, axis=0)
        rows = spread_heads(q.reshape(steps * heads, size), kv_heads).astype(BF16)
        if slot < seq_count:
            old_num, old_den = old_terms(
                rows,
                keys_ref,
                values_ref,
                lambda at: table_ref[slot, at],
                lengths_ref[replica, slot],
                KEEP_PAGES,
                0,
            )
            num = num + own_head(old_num, kv_heads)
            den = den + old_den
        else:
            last_ref[...] = rows
        num_ref[slot * steps : (slot + 1) * steps] = num.reshape(steps, heads, size)
        den_ref[slot * steps : (slot + 1) * steps] = jnp.broadcast_to(den, num.shape).reshape(
            steps, heads, size
        )


def norm_blocks_kernel(x_ref, gain_ref, out_ref):
    width = out_ref.shape[2]
    values = x_ref[...].astype(F32)
    scale = head_scale(values)
    for k, at in enumerate(half_blocks()):
        at = pl.multiple_of(at * width, 128)
        part = x_ref[:, pl.ds(at, width)].astype(F32)
        out_ref[k] = (part * scale * gain_ref[:, pl.ds(at, width)]).astype(BF16)


def half_blocks():
    replica, group = lax.axis_index("rep"), lax.axis_index("groups")
    second = jnp.where(replica < 2, 2, 1)
    third = jnp.where(replica < 2, 3, 0)
    order = [2 * replica, 2 * replica + 1]
    for source in (replica ^ 1, second, third):
        order += [2 * source + group, 2 * source + 1 - group]
    return order


def first_kernel(*refs):
    xs, (wk_ref, wv_ref), (a_ref, ya_ref, b_ref, c_ref, yb_ref, yc_ref) = refs[:4], refs[4:6], refs[6:12]
    d_ref, e_ref, acc_ref = refs[12:]
    replica = lax.axis_index("rep")
    middle = (replica == 1) | (replica == 2)
    width = wk_ref.shape[1]
    depth = a_ref.shape[0]

    def block(k):
        return jnp.concatenate([x[k] for x in xs], axis=0)

    keys, values = None, None
    for k in range(2):
        more_k = dot(block(k), wk_ref[k * depth : (k + 1) * depth])
        more_v = dot(block(k), wv_ref[k * depth : (k + 1) * depth])
        keys = more_k if keys is None else keys + more_k
        values = more_v if values is None else values + more_v
    both = dot(block(2), a_ref[...]) + dot(block(3), ya_ref[...])
    acc_ref[:, :width] = keys + both[:, :width]
    acc_ref[:, width:] = values + both[:, width:]

    @pl.when(middle)
    def _():
        acc_ref[...] += dot(block(4), b_ref[...]) + dot(block(5), yb_ref[...]) + dot(block(6), d_ref[...])

    @pl.when(jnp.logical_not(middle))
    def _():
        acc_ref[...] += dot(block(4), c_ref[...]) + dot(block(5), yc_ref[...]) + dot(block(6), e_ref[...])


def tail_kernel(far, steps, listed_ref, *refs):
    if far:
        xs, (yd_ref, ye_ref) = refs[:4], refs[4:6]
        refs = refs[6:]
    acc_ref, cos_ref, sin_ref, kgain_ref, rows_ref, num_ref, den_ref, moved_ref = refs[:8]
    keys_ref, values_ref, out_ref, o3 = refs[8:12]
    replica = lax.axis_index("rep")
    half = lax.axis_size("rep") // 2
    tokens, width = keys_ref.shape
    size = kgain_ref.shape[1]
    kv_heads = width // size
    heads = kv_heads * 8
    slots = num_ref.shape[0] // steps

    if far:
        fresh = refs[12]
        middle = (replica == 1) | (replica == 2)

        def block(k):
            return jnp.concatenate([x[k] for x in xs], axis=0)

        @pl.when(middle)
        def _():
            fresh[...] = acc_ref[...] + dot(block(7), yd_ref[...])

        @pl.when(jnp.logical_not(middle))
        def _():
            fresh[...] = acc_ref[...] + dot(block(7), ye_ref[...])

        tp, sub = lax.axis_index("tp"), lax.axis_index("sub")
        places = [tp * 2 + sub, (tp ^ 1) * 2 + sub, tp * 2 + (sub ^ 1), (tp ^ 1) * 2 + (sub ^ 1)]
    else:
        fresh, places = acc_ref, [0]
    chunk = tokens // len(places)
    for i, place in enumerate(places):
        if len(places) > 1:
            place = pl.ds(pl.multiple_of(place * chunk, chunk), chunk)
        else:
            place = pl.ds(0, chunk)
        cosine, sine = cos_ref[place, :], sin_ref[place, :]
        for h in range(kv_heads):
            x = fresh[i * chunk : (i + 1) * chunk, h * size : (h + 1) * size]
            x = rotate_rows(x * head_scale(x) * kgain_ref[...], cosine, sine)
            keys_ref[place, h * size : (h + 1) * size] = x.astype(BF16)
        values_ref[place, :] = fresh[i * chunk : (i + 1) * chunk, width:].astype(BF16)

    weights = jnp.exp(dot_rows(rows_ref[...], keys_ref[...]))
    old_num = own_head(dot(weights.astype(BF16), values_ref[...]), kv_heads)
    old_den = jnp.sum(weights, axis=-1, keepdims=True)
    at = (slots - 1) * steps
    o3[:at] = num_ref[:at] / den_ref[:at]
    o3[at:] = (num_ref[at:] + old_num.reshape(steps, heads, size)) / (
        den_ref[at:] + jnp.broadcast_to(old_den, old_num.shape).reshape(steps, heads, size)
    )
    mine = pl.ds(listed_ref[replica] * steps, steps)
    live = jnp.where(replica < half, 0.0, 1.0)
    o3[mine] = (
        live
        * (num_ref[mine] + moved_ref[0].reshape(steps, heads, size))
        / (den_ref[mine] + moved_ref[1].reshape(steps, heads, size))
    )
    for h in range(heads):
        for slot in range(slots):
            out_ref[slot, :, h * size : (h + 1) * size] = o3[
                slot * steps : (slot + 1) * steps, h, :
            ].astype(BF16)


def after(value, *others):
    return lax.optimization_barrier((value, *others))[0]


def line_pairs(pairs, axis="rep"):
    return lambda value: lax.ppermute(value, axis, pairs)


def across_groups(value, replicas):
    count = lax.axis_size("rep")
    pairs = [(g * count + r, (1 - g) * count + r) for g in range(2) for r in replicas]
    return lax.ppermute(value, ("groups", "rep"), pairs)


def diagonal(value, pairs):
    count = lax.axis_size("rep")
    pairs = [(count * g + a, count * (1 - g) + b) for g in range(2) for a, b in pairs]
    return lax.ppermute(value, ("groups", "rep"), pairs)


def body(
    rec_hidden,
    dec_hidden,
    norm_gain,
    query_gain,
    key_gain,
    w_query,
    w_key,
    w_value,
    pool_keys,
    pool_values,
    page_table,
    seq_lengths,
    listed_slot,
):
    replicas = lax.axis_size("rep")
    half = replicas // 2
    replica = lax.axis_index("rep")
    head_size = query_gain.shape[0]
    width = w_key.shape[1]
    depth = w_key.shape[0]
    _, slots, steps, features = dec_hidden.shape
    seq_count = slots - 1
    per = slots * steps
    heads = w_query.shape[1] // head_size
    gain = norm_gain[None]
    qgain, kgain = query_gain[None], key_gain[None]
    table = page_table[0]
    tokens = rec_hidden.shape[1] * lax.axis_size("tp") * lax.axis_size("sub")
    near = (
        replicas == 4
        and lax.axis_size("tp") == 2
        and lax.axis_size("sub") == 2
        and lax.axis_size("groups") == 2
    )

    rec_cos, rec_sin = rope_tables(tokens, head_size)
    flat = (per, heads, head_size)
    keys, values = pool_keys[0], pool_values[0]

    def queries(*sums):
        return call(
            functools.partial(queries_kernel, len(sums), seq_count, steps, tokens),
            [pltpu.VMEM(flat, F32)] * 3 + [pltpu.VMEM((2, steps * heads, head_size), F32)],
            [*sums, jnp.asarray(rope_freqs(head_size)), qgain, kgain, keys, values],
            [table, seq_lengths, listed_slot],
        )

    def attend(q3, k3, v3):
        return call(
            functools.partial(attend_kernel, seq_count, steps),
            [pltpu.VMEM(flat, F32)] * 2 + [pltpu.VMEM((steps * heads, width), BF16)],
            [q3, k3, v3, keys, values],
            [table, seq_lengths],
        )

    if near:
        group = lax.axis_index("groups")
        middle = (replica == 1) | (replica == 2)
        rows = depth // 2
        own = jnp.concatenate(
            [lax.dynamic_slice_in_dim(w, group * rows, rows, 0) for w in (w_key, w_value)], axis=1
        )
        spread = call(
            norm_spread_kernel, [pltpu.VMEM((per, depth), BF16)] * 4, [dec_hidden[0], gain], []
        )
        (blocks,) = call(
            norm_blocks_kernel,
            [pltpu.VMEM((2 * replicas, rec_hidden.shape[1], rows), BF16)],
            [rec_hidden[0], gain],
            [],
        )
        s1 = xor_permute(spread[1], "rep", 1)
        s2 = xor_permute(spread[2], "rep", 2)
        s3 = xor_permute(spread[3], "rep", 3)
        from_a = line_pairs([(0, 1), (1, 0), (2, 3), (3, 2)])(own)
        from_b = line_pairs([(1, 2), (2, 1)])(own)
        across = xor_permute(after(blocks, s1, s2, s3), "tp", 1)
        own_sums, pair, far_sums = project_new(
            [spread[0], s1, s2, s3], listed_slot, w_query, w_key, w_value, steps
        )
        from_d = line_pairs([(1, 2), (2, 1)])(after(from_a, from_b))
        from_c = line_pairs([(1, 0), (2, 3)])(after(from_b, from_a))
        beside = xor_permute(after(blocks, from_d, from_c), "sub", 1)
        over_a = across_groups(after(from_a, s1, s2, s3), range(4))
        over_b = across_groups(after(from_b, from_d, from_c), (1, 2))
        over_c = across_groups(from_c, (0, 3))
        pair_in = xor_permute(pair, "rep", 1)
        r2 = xor_permute((far_sums + pair_in[1].astype(F32)).astype(BF16), "rep", 2)
        from_e = line_pairs([(1, 0), (2, 3)])(after(from_d, from_c, pair_in))
        over_e = across_groups(after(from_e, across, over_a, over_b, over_c), (0, 3))
        over_d = across_groups(after(from_d, from_e, over_a, over_b, over_c), (1, 2))
        corner = xor_permute(after(across, from_e, over_a, over_b, over_c), "sub", 1)
        (acc,) = call(
            first_kernel,
            [pltpu.VMEM((tokens, 2 * width), F32)],
            [blocks, across, beside, corner, w_key, w_value, from_a, over_a, from_b, from_c, over_b, over_c, from_d, from_e],
            [],
            flops=3 * depth * tokens * width * 4,
        )
        q3, k3, v3, moved = queries(after(own_sums, acc), pair_in, r2)
        returned = lax.ppermute(moved, "rep", [(i, i + half) for i in range(half)])
        num, den, rows_last = attend(q3, k3, v3)
        far = [blocks, across, beside, corner, over_d, over_e]
    else:
        spread = lax.all_to_all(
            normalize(dec_hidden[0].reshape(per, features), norm_gain), "rep", split_axis=1, concat_axis=0, tiled=True
        ).reshape(replicas, slots, steps, depth)
        moved = jnp.take_along_axis(spread, listed_slot[:, None, None, None], axis=1)
        moved = jnp.roll(moved, half, axis=0)
        ids = jnp.arange(replicas)[:, None]
        swap = (jnp.arange(slots)[None] == listed_slot[:, None]) & (ids < half)
        spread = jnp.where(swap[:, :, None, None], moved, spread).reshape(replicas * per, depth)
        weights = jnp.concatenate([w_query, w_key, w_value], axis=1)
        sums = [
            lax.psum_scatter(
                jnp.dot(spread, weights, preferred_element_type=F32),
                "rep",
                scatter_dimension=0,
                tiled=True,
            )
        ]
        normed = lax.all_gather(
            normalize(rec_hidden[0], norm_gain), ("tp", "sub"), axis=0, tiled=True
        )
        acc = jnp.concatenate(
            [
                jnp.dot(
                    normed,
                    lax.all_gather(w, "rep", axis=0, tiled=True),
                    preferred_element_type=F32,
                )
                for w in (w_key, w_value)
            ],
            axis=1,
        )
        far = []
        q3, k3, v3, moved = queries(*sums)
        returned = lax.ppermute(moved, "rep", [(i, i + half) for i in range(half)])
        num, den, rows_last = attend(q3, k3, v3)

    rec_k, rec_v, decoded = call(
        functools.partial(tail_kernel, bool(far), steps),
        [
            shaped((tokens, width), BF16),
            shaped((tokens, width), BF16),
            shaped((slots, steps, heads * head_size), BF16),
        ],
        [*far, acc, rec_cos, rec_sin, kgain, rows_last, num, den, returned],
        [listed_slot],
        scratch=[pltpu.VMEM(flat, F32)] + [pltpu.VMEM((tokens, 2 * width), F32)] * bool(far),
        flops=depth * tokens * width * 4,
    )
    return (rec_k[None], rec_v[None], decoded[None])


def solution(mesh):
    in_specs = (
        P(("groups", "rep"), ("tp", "sub"), None),
        P(("groups", "rep"), None, None, None),
        P(),
        P(),
        P(),
        P("rep", ("tp", "sub")),
        P("rep", ("tp", "sub")),
        P("rep", ("tp", "sub")),
        P(("groups", "rep"), None, None, ("tp", "sub")),
        P(("groups", "rep"), None, None, ("tp", "sub")),
        P(("groups", "rep"), None, None),
        P("groups", None),
        P("groups"),
    )
    out_specs = (
        P(("groups", "rep"), None, ("tp", "sub")),
        P(("groups", "rep"), None, ("tp", "sub")),
        P(("groups", "rep"), None, None, ("tp", "sub")),
    )
    return jax.shard_map(body, mesh=mesh, in_specs=in_specs, out_specs=out_specs, check_vma=False)
```

```python
import functools
import math

import jax
import jax.numpy as jnp
import numpy as np
from jax import lax
from jax.experimental import pallas as pl
from jax.experimental.pallas import tpu as pltpu
from jax.sharding import PartitionSpec as P

EPSILON = 1e-06
ROPE_BASE = 1000000.0
KEEP_PAGES = 3
VMEM_BYTES = 16 * 2**20
F32 = jnp.float32
BF16 = jnp.bfloat16

WHOLE = pl.BlockSpec(memory_space=pltpu.VMEM)
SCALAR = pl.BlockSpec(memory_space=pltpu.SMEM)


def call(kernel, outs, ins, scalars, scratch=(), flops=0):
    bytes_accessed = sum(math.prod(a.shape) * a.dtype.itemsize for a in list(ins) + list(outs))
    return pl.pallas_call(
        kernel,
        out_shape=tuple(outs),
        in_specs=[SCALAR] * len(scalars) + [WHOLE] * len(ins),
        out_specs=tuple([WHOLE] * len(outs)),
        scratch_shapes=list(scratch),
        compiler_params=pltpu.CompilerParams(vmem_limit_bytes=VMEM_BYTES),
        cost_estimate=pl.CostEstimate(flops=flops, bytes_accessed=bytes_accessed, transcendentals=0),
    )(*scalars, *[pltpu.with_memory_space_constraint(a, pltpu.VMEM) for a in ins])


def shaped(shape, dtype):
    return jax.ShapeDtypeStruct(shape, dtype)


def dot(a, b):
    return jnp.dot(a, b, preferred_element_type=F32)


def dot_rows(a, b):
    return lax.dot_general(a, b, (((1,), (1,)), ((), ())), preferred_element_type=F32)


def xor_permute(value, axis, distance):
    count = lax.axis_size(axis)
    return lax.ppermute(value, axis, [(i, i ^ distance) for i in range(count)])


def head_scale(values):
    return lax.rsqrt(jnp.mean(values * values, axis=-1, keepdims=True) + EPSILON)


def rotate_rows(values, cosine, sine):
    return values * cosine + pltpu.roll(values, values.shape[-1] // 2, values.ndim - 1) * sine


def rope_freqs(head_size):
    half = np.arange(head_size // 2, dtype=np.float32)
    freqs = np.exp(half * np.float32(-2.0 * math.log(ROPE_BASE) / head_size)).astype(np.float32)
    return np.concatenate([freqs, freqs])[None]


def rope_tables(count, head_size):
    angles = np.arange(count, dtype=np.float32)[:, None] * rope_freqs(head_size)
    signs = np.where(np.arange(head_size) < head_size // 2, -1.0, 1.0)
    cosine, sine = np.cos(angles.astype(np.float64)), np.sin(angles.astype(np.float64)) * signs
    return jnp.asarray(cosine, F32), jnp.asarray(sine, F32)


def normalize(states, gain):
    values = states.astype(F32)
    return (values * head_scale(values) * gain).astype(BF16)


def norm_spread_kernel(x_ref, gain_ref, *outs):
    replica = lax.axis_index("rep")
    slots, steps, _ = x_ref.shape
    width = outs[0].shape[1]
    for slot in range(slots):
        values = x_ref[slot].astype(F32)
        scale = head_scale(values)
        for k, out in enumerate(outs):
            at = pl.multiple_of((replica ^ k) * width, 128)
            part = x_ref[slot, :, pl.ds(at, width)].astype(F32)
            out[slot * steps : (slot + 1) * steps, :] = (
                part * scale * gain_ref[:, pl.ds(at, width)]
            ).astype(BF16)


def project_kernel(count, steps, listed_ref, *refs):
    rows = refs[:count]
    wq_ref, wk_ref, wv_ref, own_ref = refs[count : count + 4]
    pair_ref, far_ref, stacked = refs[count + 4 :]
    replica = lax.axis_index("rep")
    half = count // 2
    per = rows[0].shape[0]
    pad = stacked.shape[1]
    ids = lax.broadcasted_iota(jnp.int32, (per, 1), 0)
    for k in range(count):
        own = rows[k][...].astype(F32)
        other = rows[k ^ half][...].astype(F32)
        busy = (replica ^ k) < half
        for t in range(steps):
            from_row = ids == listed_ref[replica ^ k ^ half] * steps + t
            moved = jnp.sum(jnp.where(from_row, other, 0.0), axis=0, keepdims=True)
            own = jnp.where((ids == listed_ref[replica ^ k] * steps + t) & busy, moved, own)
        stacked[k, :per, :] = own.astype(BF16)
    lhs = stacked[...].reshape(-1, stacked.shape[2])
    width = wk_ref.shape[1]
    at = 0
    for w_ref, pieces in ((wq_ref, wq_ref.shape[1] // width), (wk_ref, 1), (wv_ref, 1)):
        for piece in range(pieces):
            product = dot(lhs, w_ref[:, piece * width : (piece + 1) * width])
            own_ref[:, at : at + width] = product[:per]
            for i, k in enumerate((1, 3)):
                pair_ref[i, :, at : at + width] = product[k * pad : k * pad + per].astype(BF16)
            far_ref[:, at : at + width] = product[2 * pad : 2 * pad + per]
            at += width


def project_new(rows, listed, w_query, w_key, w_value, steps):
    count = len(rows)
    per, depth = rows[0].shape
    pad = -(-per // 16) * 16
    total = w_query.shape[1] + 2 * w_key.shape[1]
    return call(
        functools.partial(project_kernel, count, steps),
        [
            pltpu.VMEM((per, total), F32),
            pltpu.VMEM((2, per, total), BF16),
            pltpu.VMEM((per, total), F32),
        ],
        [*rows, w_query, w_key, w_value],
        [listed],
        scratch=[pltpu.VMEM((count, pad, depth), BF16)],
        flops=2 * count * per * depth * total,
    )


def spread_heads(rows, kv_heads):
    heads = kv_heads * 8
    ids = lax.broadcasted_iota(jnp.int32, (rows.shape[0], 1), 0) % heads // 8
    return jnp.concatenate([jnp.where(ids == k, rows, 0.0) for k in range(kv_heads)], axis=1)


def own_head(wide, kv_heads):
    size = wide.shape[1] // kv_heads
    heads = kv_heads * 8
    ids = lax.broadcasted_iota(jnp.int32, (wide.shape[0], 1), 0) % heads // 8
    total = wide[:, :size]
    for k in range(1, kv_heads):
        total = jnp.where(ids == k, wide[:, k * size : (k + 1) * size], total)
    return total


def old_terms(rows, keys_ref, values_ref, page_of, length, pages, first):
    page = keys_ref.shape[1]
    keys = jnp.concatenate([keys_ref[page_of(first + i)] for i in range(pages)], axis=0)
    values = jnp.concatenate([values_ref[page_of(first + i)] for i in range(pages)], axis=0)
    scores = dot_rows(rows, keys)
    ids = lax.broadcasted_iota(jnp.int32, scores.shape, 1) + first * page
    weights = jnp.where(ids < length, jnp.exp(scores), 0.0)
    return dot(weights.astype(BF16), values), jnp.sum(weights, axis=-1, keepdims=True)


def queries_kernel(parts, seq_count, steps, tokens, table_ref, lengths_ref, listed_ref, *refs):
    sums = refs[:parts]
    freqs_ref, qgain_ref, kgain_ref, keys_ref, values_ref = refs[parts : parts + 5]
    q3, k3, v3, moved_ref = refs[parts + 5 :]
    replica = lax.axis_index("rep")
    half = lax.axis_size("rep") // 2
    size = qgain_ref.shape[1]
    width = keys_ref.shape[2]
    kv_heads = width // size
    heads = kv_heads * 8
    slots = seq_count + 1
    per = slots * steps

    def total(at):
        value = sums[0][:, at : at + size].astype(F32)
        for other in sums[1:]:
            part = other[0] if len(other.shape) == 3 else other[...]
            value = value + part[:, at : at + size].astype(F32)
        return value

    partner = jnp.where(replica < half, replica, replica - half)
    arrived = lengths_ref[partner, listed_ref[partner]]
    ids = lax.broadcasted_iota(jnp.int32, (per, 1), 0)
    positions = ids % steps
    for slot in range(slots):
        base = tokens
        if slot < seq_count:
            base = jnp.where(listed_ref[replica] == slot, arrived, lengths_ref[replica, slot])
        positions = positions + jnp.where(ids // steps == slot, base, 0)
    angles = positions.astype(F32) * freqs_ref[...]
    lanes = lax.broadcasted_iota(jnp.int32, (per, size), 1)
    cosine, sine = jnp.cos(angles), jnp.sin(angles)
    sine = jnp.where(lanes < size // 2, -sine, sine)

    for h in range(heads):
        x = total(h * size)
        x = rotate_rows(x * head_scale(x) * qgain_ref[...], cosine, sine) * size**-0.5
        q3[:, h, :] = x.astype(BF16).astype(F32)
    for h in range(kv_heads):
        x = total((heads + h) * size)
        x = rotate_rows(x * head_scale(x) * kgain_ref[...], cosine, sine).astype(BF16).astype(F32)
        k3[:, h * 8 : h * 8 + 8, :] = jnp.broadcast_to(x[:, None, :], (per, 8, size))
        v = total((heads + kv_heads + h) * size).astype(BF16).astype(F32)
        v3[:, h * 8 : h * 8 + 8, :] = jnp.broadcast_to(v[:, None, :], (per, 8, size))

    moved_ref[...] = jnp.zeros_like(moved_ref)

    @pl.when(replica < half)
    def _():
        slot = listed_ref[replica]
        length = lengths_ref[replica, slot]
        rows = q3[pl.ds(slot * steps, steps)].reshape(steps * heads, size)
        rows = spread_heads(rows, kv_heads).astype(BF16)
        num, den = old_terms(
            rows, keys_ref, values_ref, lambda at: table_ref[slot, at], length, table_ref.shape[1], 0
        )
        num = own_head(num, kv_heads)
        moved_ref[0] = num
        moved_ref[1] = jnp.broadcast_to(den, num.shape)


def attend_kernel(seq_count, steps, table_ref, lengths_ref, *refs):
    q3, k3, v3, keys_ref, values_ref, num_ref, den_ref, last_ref = refs
    replica = lax.axis_index("rep")
    heads, size = q3.shape[1:]
    kv_heads = keys_ref.shape[2] // size
    for slot in range(seq_count + 1):
        q = q3[slot * steps : (slot + 1) * steps]
        k = k3[slot * steps : (slot + 1) * steps]
        v = v3[slot * steps : (slot + 1) * steps]
        nums, dens = [], []
        for t in range(steps):
            num, den = None, None
            for u in range(t + 1):
                e = jnp.exp(jnp.sum(q[t] * k[u], axis=-1, keepdims=True))
                num = e * v[u] if num is None else num + e * v[u]
                den = e if den is None else den + e
            nums.append(num)
            dens.append(den)
        num, den = jnp.concatenate(nums, axis=0), jnp.concatenate(dens, axis=0)
        rows = spread_heads(q.reshape(steps * heads, size), kv_heads).astype(BF16)
        if slot < seq_count:
            old_num, old_den = old_terms(
                rows,
                keys_ref,
                values_ref,
                lambda at: table_ref[slot, at],
                lengths_ref[replica, slot],
                KEEP_PAGES,
                0,
            )
            num = num + own_head(old_num, kv_heads)
            den = den + old_den
        else:
            last_ref[...] = rows
        num_ref[slot * steps : (slot + 1) * steps] = num.reshape(steps, heads, size)
        den_ref[slot * steps : (slot + 1) * steps] = jnp.broadcast_to(den, num.shape).reshape(
            steps, heads, size
        )


def norm_blocks_kernel(x_ref, gain_ref, out_ref):
    width = out_ref.shape[2]
    values = x_ref[...].astype(F32)
    scale = head_scale(values)
    for k, at in enumerate(half_blocks()):
        at = pl.multiple_of(at * width, 128)
        part = x_ref[:, pl.ds(at, width)].astype(F32)
        out_ref[k] = (part * scale * gain_ref[:, pl.ds(at, width)]).astype(BF16)


def half_blocks():
    replica, group = lax.axis_index("rep"), lax.axis_index("groups")
    second = jnp.where(replica < 2, 2, 1)
    third = jnp.where(replica < 2, 3, 0)
    order = [2 * replica, 2 * replica + 1]
    for source in (replica ^ 1, second, third):
        order += [2 * source + group, 2 * source + 1 - group]
    return order


def first_kernel(*refs):
    xs, (wk_ref, wv_ref), (a_ref, ya_ref, b_ref, c_ref, yb_ref, yc_ref) = refs[:4], refs[4:6], refs[6:12]
    d_ref, e_ref, acc_ref = refs[12:]
    replica = lax.axis_index("rep")
    middle = (replica == 1) | (replica == 2)
    width = wk_ref.shape[1]
    depth = a_ref.shape[0]

    def block(k):
        return jnp.concatenate([x[k] for x in xs], axis=0)

    keys, values = None, None
    for k in range(2):
        more_k = dot(block(k), wk_ref[k * depth : (k + 1) * depth])
        more_v = dot(block(k), wv_ref[k * depth : (k + 1) * depth])
        keys = more_k if keys is None else keys + more_k
        values = more_v if values is None else values + more_v
    both = dot(block(2), a_ref[...]) + dot(block(3), ya_ref[...])
    acc_ref[:, :width] = keys + both[:, :width]
    acc_ref[:, width:] = values + both[:, width:]

    @pl.when(middle)
    def _():
        acc_ref[...] += dot(block(4), b_ref[...]) + dot(block(5), yb_ref[...]) + dot(block(6), d_ref[...])

    @pl.when(jnp.logical_not(middle))
    def _():
        acc_ref[...] += dot(block(4), c_ref[...]) + dot(block(5), yc_ref[...]) + dot(block(6), e_ref[...])


def tail_kernel(far, steps, listed_ref, *refs):
    if far:
        xs, (yd_ref, ye_ref) = refs[:4], refs[4:6]
        refs = refs[6:]
    acc_ref, cos_ref, sin_ref, kgain_ref, rows_ref, num_ref, den_ref, moved_ref = refs[:8]
    keys_ref, values_ref, out_ref, o3 = refs[8:12]
    replica = lax.axis_index("rep")
    half = lax.axis_size("rep") // 2
    tokens, width = keys_ref.shape
    size = kgain_ref.shape[1]
    kv_heads = width // size
    heads = kv_heads * 8
    slots = num_ref.shape[0] // steps

    if far:
        fresh = refs[12]
        middle = (replica == 1) | (replica == 2)

        def block(k):
            return jnp.concatenate([x[k] for x in xs], axis=0)

        @pl.when(middle)
        def _():
            fresh[...] = acc_ref[...] + dot(block(7), yd_ref[...])

        @pl.when(jnp.logical_not(middle))
        def _():
            fresh[...] = acc_ref[...] + dot(block(7), ye_ref[...])

        tp, sub = lax.axis_index("tp"), lax.axis_index("sub")
        places = [tp * 2 + sub, (tp ^ 1) * 2 + sub, tp * 2 + (sub ^ 1), (tp ^ 1) * 2 + (sub ^ 1)]
    else:
        fresh, places = acc_ref, [0]
    chunk = tokens // len(places)
    for i, place in enumerate(places):
        if len(places) > 1:
            place = pl.ds(pl.multiple_of(place * chunk, chunk), chunk)
        else:
            place = pl.ds(0, chunk)
        cosine, sine = cos_ref[place, :], sin_ref[place, :]
        for h in range(kv_heads):
            x = fresh[i * chunk : (i + 1) * chunk, h * size : (h + 1) * size]
            x = rotate_rows(x * head_scale(x) * kgain_ref[...], cosine, sine)
            keys_ref[place, h * size : (h + 1) * size] = x.astype(BF16)
        values_ref[place, :] = fresh[i * chunk : (i + 1) * chunk, width:].astype(BF16)

    weights = jnp.exp(dot_rows(rows_ref[...], keys_ref[...]))
    old_num = own_head(dot(weights.astype(BF16), values_ref[...]), kv_heads)
    old_den = jnp.sum(weights, axis=-1, keepdims=True)
    at = (slots - 1) * steps
    o3[:at] = num_ref[:at] / den_ref[:at]
    o3[at:] = (num_ref[at:] + old_num.reshape(steps, heads, size)) / (
        den_ref[at:] + jnp.broadcast_to(old_den, old_num.shape).reshape(steps, heads, size)
    )
    mine = pl.ds(listed_ref[replica] * steps, steps)
    live = jnp.where(replica < half, 0.0, 1.0)
    o3[mine] = (
        live
        * (num_ref[mine] + moved_ref[0].reshape(steps, heads, size))
        / (den_ref[mine] + moved_ref[1].reshape(steps, heads, size))
    )
    for h in range(heads):
        for slot in range(slots):
            out_ref[slot, :, h * size : (h + 1) * size] = o3[
                slot * steps : (slot + 1) * steps, h, :
            ].astype(BF16)


def after(value, *others):
    return lax.optimization_barrier((value, *others))[0]


def line_pairs(pairs, axis="rep"):
    return lambda value: lax.ppermute(value, axis, pairs)


def across_groups(value, replicas):
    count = lax.axis_size("rep")
    pairs = [(g * count + r, (1 - g) * count + r) for g in range(2) for r in replicas]
    return lax.ppermute(value, ("groups", "rep"), pairs)


def diagonal(value, pairs):
    count = lax.axis_size("rep")
    pairs = [(count * g + a, count * (1 - g) + b) for g in range(2) for a, b in pairs]
    return lax.ppermute(value, ("groups", "rep"), pairs)


def body(
    rec_hidden,
    dec_hidden,
    norm_gain,
    query_gain,
    key_gain,
    w_query,
    w_key,
    w_value,
    pool_keys,
    pool_values,
    page_table,
    seq_lengths,
    listed_slot,
):
    replicas = lax.axis_size("rep")
    half = replicas // 2
    replica = lax.axis_index("rep")
    head_size = query_gain.shape[0]
    width = w_key.shape[1]
    depth = w_key.shape[0]
    _, slots, steps, features = dec_hidden.shape
    seq_count = slots - 1
    per = slots * steps
    heads = w_query.shape[1] // head_size
    gain = norm_gain[None]
    qgain, kgain = query_gain[None], key_gain[None]
    table = page_table[0]
    tokens = rec_hidden.shape[1] * lax.axis_size("tp") * lax.axis_size("sub")
    near = (
        replicas == 4
        and lax.axis_size("tp") == 2
        and lax.axis_size("sub") == 2
        and lax.axis_size("groups") == 2
    )

    rec_cos, rec_sin = rope_tables(tokens, head_size)
    flat = (per, heads, head_size)
    keys, values = pool_keys[0], pool_values[0]

    def queries(*sums):
        return call(
            functools.partial(queries_kernel, len(sums), seq_count, steps, tokens),
            [pltpu.VMEM(flat, F32)] * 3 + [pltpu.VMEM((2, steps * heads, head_size), F32)],
            [*sums, jnp.asarray(rope_freqs(head_size)), qgain, kgain, keys, values],
            [table, seq_lengths, listed_slot],
        )

    def attend(q3, k3, v3):
        return call(
            functools.partial(attend_kernel, seq_count, steps),
            [pltpu.VMEM(flat, F32)] * 2 + [pltpu.VMEM((steps * heads, width), BF16)],
            [q3, k3, v3, keys, values],
            [table, seq_lengths],
        )

    if near:
        group = lax.axis_index("groups")
        middle = (replica == 1) | (replica == 2)
        rows = depth // 2
        own = jnp.concatenate(
            [lax.dynamic_slice_in_dim(w, group * rows, rows, 0) for w in (w_key, w_value)], axis=1
        )
        spread = call(
            norm_spread_kernel, [pltpu.VMEM((per, depth), BF16)] * 4, [dec_hidden[0], gain], []
        )
        (blocks,) = call(
            norm_blocks_kernel,
            [pltpu.VMEM((2 * replicas, rec_hidden.shape[1], rows), BF16)],
            [rec_hidden[0], gain],
            [],
        )
        s1 = xor_permute(spread[1], "rep", 1)
        s2 = xor_permute(spread[2], "rep", 2)
        s3 = xor_permute(spread[3], "rep", 3)
        from_a = line_pairs([(0, 1), (1, 0), (2, 3), (3, 2)])(own)
        from_b = line_pairs([(1, 2), (2, 1)])(own)
        across = xor_permute(after(blocks, s1, s2, s3), "tp", 1)
        own_sums, pair, far_sums = project_new(
            [spread[0], s1, s2, s3], listed_slot, w_query, w_key, w_value, steps
        )
        from_d = line_pairs([(1, 2), (2, 1)])(after(from_a, from_b))
        from_c = line_pairs([(1, 0), (2, 3)])(after(from_b, from_a))
        beside = xor_permute(after(blocks, from_d, from_c), "sub", 1)
        over_a = across_groups(after(from_a, s1, s2, s3), range(4))
        over_b = across_groups(after(from_b, from_d, from_c), (1, 2))
        over_c = across_groups(from_c, (0, 3))
        pair_in = xor_permute(pair, "rep", 1)
        r2 = xor_permute((far_sums + pair_in[1].astype(F32)).astype(BF16), "rep", 2)
        from_e = line_pairs([(1, 0), (2, 3)])(after(from_d, from_c, pair_in))
        over_e = across_groups(after(from_e, across, over_a, over_b, over_c), (0, 3))
        over_d = across_groups(after(from_d, from_e, over_a, over_b, over_c), (1, 2))
        corner = xor_permute(after(across, from_e, over_a, over_b, over_c), "sub", 1)
        (acc,) = call(
            first_kernel,
            [pltpu.VMEM((tokens, 2 * width), F32)],
            [blocks, across, beside, corner, w_key, w_value, from_a, over_a, from_b, from_c, over_b, over_c, from_d, from_e],
            [],
            flops=3 * depth * tokens * width * 4,
        )
        q3, k3, v3, moved = queries(after(own_sums, acc), pair_in, r2)
        returned = lax.ppermute(moved, "rep", [(i, i + half) for i in range(half)])
        num, den, rows_last = attend(q3, k3, v3)
        far = [blocks, across, beside, corner, over_d, over_e]
    else:
        spread = lax.all_to_all(
            normalize(dec_hidden[0].reshape(per, features), norm_gain), "rep", split_axis=1, concat_axis=0, tiled=True
        ).reshape(replicas, slots, steps, depth)
        moved = jnp.take_along_axis(spread, listed_slot[:, None, None, None], axis=1)
        moved = jnp.roll(moved, half, axis=0)
        ids = jnp.arange(replicas)[:, None]
        swap = (jnp.arange(slots)[None] == listed_slot[:, None]) & (ids < half)
        spread = jnp.where(swap[:, :, None, None], moved, spread).reshape(replicas * per, depth)
        weights = jnp.concatenate([w_query, w_key, w_value], axis=1)
        sums = [
            lax.psum_scatter(
                jnp.dot(spread, weights, preferred_element_type=F32),
                "rep",
                scatter_dimension=0,
                tiled=True,
            )
        ]
        normed = lax.all_gather(
            normalize(rec_hidden[0], norm_gain), ("tp", "sub"), axis=0, tiled=True
        )
        acc = jnp.concatenate(
            [
                jnp.dot(
                    normed,
                    lax.all_gather(w, "rep", axis=0, tiled=True),
                    preferred_element_type=F32,
                )
                for w in (w_key, w_value)
            ],
            axis=1,
        )
        far = []
        q3, k3, v3, moved = queries(*sums)
        returned = lax.ppermute(moved, "rep", [(i, i + half) for i in range(half)])
        num, den, rows_last = attend(q3, k3, v3)

    rec_k, rec_v, decoded = call(
        functools.partial(tail_kernel, bool(far), steps),
        [
            shaped((tokens, width), BF16),
            shaped((tokens, width), BF16),
            shaped((slots, steps, heads * head_size), BF16),
        ],
        [*far, acc, rec_cos, rec_sin, kgain, rows_last, num, den, returned],
        [listed_slot],
        scratch=[pltpu.VMEM(flat, F32)] + [pltpu.VMEM((tokens, 2 * width), F32)] * bool(far),
        flops=depth * tokens * width * 4,
    )
    return (rec_k[None], rec_v[None], decoded[None])


def solution(mesh):
    in_specs = (
        P(("groups", "rep"), ("tp", "sub"), None),
        P(("groups", "rep"), None, None, None),
        P(),
        P(),
        P(),
        P("rep", ("tp", "sub")),
        P("rep", ("tp", "sub")),
        P("rep", ("tp", "sub")),
        P(("groups", "rep"), None, None, ("tp", "sub")),
        P(("groups", "rep"), None, None, ("tp", "sub")),
        P(("groups", "rep"), None, None),
        P("groups", None),
        P("groups"),
    )
    out_specs = (
        P(("groups", "rep"), None, ("tp", "sub")),
        P(("groups", "rep"), None, ("tp", "sub")),
        P(("groups", "rep"), None, None, ("tp", "sub")),
    )
    return jax.shard_map(body, mesh=mesh, in_specs=in_specs, out_specs=out_specs, check_vma=False)
```
